256 devices in a mesh: band: 32 (over x, y, core), sub: 8 (over z).
Axes of the slice: x: 4, y: 4, z: 8, core: 2. Of those that a mesh axis runs over, the one named last changes fastest.
Arguments:
- panels: bfloat16 [32, 8, 32, 256, 256], P('band', 'sub'), may hold values from -0.375 to 0.375
- chain_map: float32 [32, 256, 256], P('band'), as said below
- couplers: bfloat16 [32, 8, 32, 16, 256], P('band', 'sub'), may hold values from -0.375 to 0.375
- anc_band: int32 [8192, 4], P(('band', 'sub')), may hold values from 0 to 31, all different within a row; in each aligned block of 32 rows (0 to 31, 32 to 63, ...) at most 8 rows name the same one
- anc_slot: int32 [8192, 4], P(('band', 'sub')), may hold values from 0 to 31
Outputs:
- front: float32 [32, 256, 256], P('band')
- grads: float32 [32, 8, 32, 16, 256], P('band', 'sub')
The draws below stay inside these ranges and needn't reach their ends.
Inputs may be any that keep to these rules, and one draw needn't show every extreme that they name: Each row of anc_band lists 4 different bands; among the 32 rows of one device no band is named more than 8 times, a bound that some block reaches. `chain_map`: each band's matrix is a diagonal of entries in (0.5, 0.98) plus small dense off-diagonal entries.
All inputs are finite; a program needn't handle non-finite values.
Results may differ from the reference program's by a relative error of at most 0.0026.
Values may be sent and summed in bfloat16 or wider, within the bound.
A program may use at most 64 MiB of HBM per device.

```python
import math
import jax
import jax.numpy as jnp
import numpy as np
from jax import lax

W = 256
NS = 32
R = 16
K = 4
CAP = 8
ROWS = 8192
N_BAND = 32
N_SUB = 8


def draw_chain_map(key, part):
    key = jax.random.fold_in(key, 7)
    first, second = jax.random.split(key)
    decay = jnp.exp(jax.random.uniform(first, (N_BAND, W, 1), jnp.float32, jnp.log(0.5), jnp.log(0.98)))
    noise = jax.random.normal(second, (N_BAND, W, W), jnp.float32) * (0.08 / W ** 0.5)
    eye = (jnp.arange(W)[:, None] == jnp.arange(W)[None, :]).astype(jnp.float32)
    return decay * eye + noise * (1.0 - eye)


def plant(entries, key, low, high):
    extent = entries.shape
    place = [jax.random.randint(jax.random.fold_in(key, axis), (), 0, extent[axis]) for axis in range(len(extent))]
    entries = entries.at[tuple(place)].set(low)
    longest = extent.index(max(extent))
    place[longest] = (place[longest] + 1) % extent[longest]
    return entries.at[tuple(place)].set(high)


def level_of(own_key, dims, cuts, smallest, top_value):
    def one(dim, shards_of):
        steps = jax.random.uniform(jax.random.fold_in(jax.random.fold_in(own_key, 6), dim), (shards_of,), jnp.float32, smallest / len(cuts), top_value / len(cuts))
        return jnp.repeat(jnp.exp(steps), dims[dim] // shards_of).reshape((-1,) + (1,) * (len(dims) - dim - 1))

    loudness = one(*cuts[0])
    for cut in cuts[1:]:
        loudness = loudness * one(*cut)
    return loudness


def deal_out(stream_key, own, number, rows, count, top, most, skew):
    order = jax.random.permutation(stream_key, count)
    crowded, common = portions_of(count, rows * top, most, skew, True), portions_of(count, rows * top, most, skew, False)
    places = jnp.arange(count)

    def named(lengths, rotation):
        used = int((lengths > 0).sum())
        fixed = max(1, used // 4)
        moved = fixed + (places - fixed + rotation * (used - fixed)) % max(1, count - fixed)
        return jnp.zeros((count,), jnp.int32).at[order[jnp.where(places < fixed, places, moved)]].set(jnp.asarray(lengths, jnp.int32))

    lengths = jnp.where(number % 4 == 0, named(crowded, number // 4), named(common, number - number // 4 - 1))
    mixed = jax.random.permutation(jax.random.fold_in(own, 3), count)
    donor, taker = mixed[0:count // 2 * 2:2], mixed[1:count // 2 * 2:2]
    slack = jnp.minimum(lengths[donor] - 1, most - lengths[taker]) // 2
    slack = jnp.where((donor == order[0]) | (taker == order[0]) | (lengths[taker] == 0), 0, jnp.maximum(slack, 0))
    moved = jax.random.randint(jax.random.fold_in(own, 4), (count // 2,), 0, 1 << 20) % (slack + 1)
    lengths = lengths.at[donor].add(-moved).at[taker].add(moved)
    labels = jnp.searchsorted(jnp.cumsum(lengths), jnp.arange(rows * top), side="right").astype(jnp.int32)
    grid = labels.reshape(top, rows).T
    grid = grid[jax.random.permutation(jax.random.fold_in(own, 1), rows)]
    rotation = jax.random.randint(jax.random.fold_in(own, 2), (rows, 1), 0, top)
    return jnp.take_along_axis(grid, (jnp.arange(top)[None, :] + rotation) % top, axis=1)


def portions_of(amount, total, reach, lean, full):
    portions = [(1 << 20) // math.isqrt(rank ** lean) + 1 for rank in range(1, amount + 1)]
    largest = reach if full else min(reach, max(-(-total // amount), total * portions[0] // sum(portions)))
    least = 1 if total - largest >= amount - 1 else 0
    given, rest = [largest] + [least] * (amount - 1), total - largest - least * (amount - 1)
    while rest > 0:
        movable = [i for i in range(1, amount) if given[i] < largest] or [i for i in range(1, amount) if given[i] < reach]
        mass, remaining = sum([portions[i] for i in movable]), rest
        for i in movable:
            addition = min(reach - given[i], max(1, remaining * portions[i] // mass), rest)
            given[i] = given[i] + addition
            rest = rest - addition
    return np.array(given)


def scatter_about(own_key, extent, spread, bound, cuts=(), kind=jnp.bfloat16):
    factor_of = level_of(own_key, extent, cuts, -0.22, 0.18) if cuts else 1.0
    values = jax.random.normal(own_key, extent, jnp.float32) * spread * factor_of
    return jnp.minimum(jnp.maximum(values, -bound), bound).astype(kind)


def setup_inputs(seed: int = 0) -> dict:
    splits = jax.random.split(jax.random.key(seed), 6)
    panels = scatter_about(splits[0], (N_BAND, N_SUB, NS, W, W), W ** -0.5, 0.375, ((0, 32), (1, 8)))
    chain_map = draw_chain_map(jax.random.fold_in(splits[5], 71), 0)
    couplers = scatter_about(splits[2], (N_BAND, N_SUB, NS, R, W), W ** -0.5, 0.375, ((0, 32), (1, 8)))
    anc_band_keys = jax.random.split(jax.random.fold_in(splits[3], 1), ROWS // NS)
    anc_band_turns = jax.random.permutation(jax.random.fold_in(splits[3], 3), ROWS // NS)
    anc_band = jax.vmap(lambda own, number: deal_out(jax.random.fold_in(splits[3], 2), own, number, NS, N_BAND, K, CAP, 2))(anc_band_keys, anc_band_turns).reshape((ROWS, K))
    anc_slot = plant(jax.random.randint(splits[4], (ROWS, K), 0, NS), jax.random.fold_in(splits[4], 1), 0, NS - 1).astype(jnp.int32)
    return dict(panels=panels, chain_map=chain_map, couplers=couplers, anc_band=anc_band, anc_slot=anc_slot)


def reference(panels, chain_map, couplers, anc_band, anc_slot):
    hi = lax.Precision.HIGHEST

    def band_update(block):
        flat = block.reshape(N_SUB * NS, W, W).astype(jnp.float32)
        gram = jnp.einsum('nik,nil->kl', flat, flat, precision=hi)
        return gram / (N_SUB * NS)

    update = lax.map(band_update, panels)

    def chain_step(state, pieces):
        upd, mat = pieces
        nxt = upd + jnp.dot(jnp.dot(mat, state, precision=hi), mat.T, precision=hi)
        return nxt, state

    _, front = lax.scan(chain_step, jnp.zeros((W, W), jnp.float32), (update, chain_map))

    def band_adjoint(pieces):
        block, coup, state = pieces
        coupled = jnp.einsum('sjrk,sjkl->sjrl', coup.astype(jnp.float32), block.astype(jnp.float32), precision=hi)
        return jnp.einsum('sjrk,kl->sjrl', coupled, state, precision=hi)

    adjoint = lax.map(band_adjoint, (panels, couplers, front))
    sent = adjoint.astype(jnp.bfloat16).astype(jnp.float32).reshape(N_BAND * N_SUB * NS, R * W)
    rows = jnp.arange(N_BAND * N_SUB * NS, dtype=jnp.int32)
    source_sub = (rows // NS) % N_SUB
    target = (anc_band * N_SUB + source_sub[:, None]) * NS + anc_slot
    repeated = jnp.repeat(sent, K, axis=0)
    received = jax.ops.segment_sum(repeated, target.reshape(-1), num_segments=N_BAND * N_SUB * NS)
    grads = adjoint + received.reshape(N_BAND, N_SUB, NS, R, W)
    return front, grads
```

```python
import functools

import jax
import jax.numpy as jnp
from jax import lax
from jax.experimental import pallas as pl
from jax.experimental.pallas import tpu as pltpu
from jax.sharding import PartitionSpec as P

MESH = pl.DeviceIdType.MESH
F32, BF16 = jnp.float32, jnp.bfloat16
CHIPS_X, CHIPS_Y = 4, 4
PAD = 16


def split(value):
    high = value.astype(BF16)
    return high, (value - high.astype(F32)).astype(BF16)


def dot(a, b):
    return jnp.dot(a, b, preferred_element_type=F32)


def dot_t(a, b):
    return lax.dot_general(a, b, (((1,), (1,)), ((), ())), preferred_element_type=F32)


def product(a, b):
    ah, al = split(a)
    bh, bl = split(b)
    return dot(ah, bh) + (dot(ah, bl) + dot(al, bh))


def diagonal(width):
    rows = lax.broadcasted_iota(jnp.int32, (width, width), 0)
    return rows == lax.broadcasted_iota(jnp.int32, (width, width), 1)


def pack(value, message):
    width = value.shape[1]
    high = value.astype(BF16)
    rest = jnp.where(diagonal(width), value - high.astype(F32), 0.0)
    message[0:width, :] = high
    rest = jnp.sum(rest, axis=0, keepdims=True)
    message[width : width + PAD, :] = jnp.broadcast_to(rest, (PAD, width)).astype(BF16)


def unpack(message):
    width = message.shape[1]
    rest = message[width : width + PAD, :].astype(F32)[0:1, :]
    return message[0:width, :].astype(F32) + jnp.where(diagonal(width), rest, 0.0)


def kernel(
    nx, ny, nz, ns, nr,
    panels, map_ref, coup_ref, key_ref,
    front_ref, grads_ref,
    pv, gram, rsbuf, upd, upd_other, map_other, abuf, bbuf, vbuf, tbuf,
    tcat, kcat, wcat, ycat, crm, cjm, gacc, ccat, fcat,
    keys0, keys1, x0, x1, o0, o1, rb0, rb1,
    psem, rs_s, rs_r, ag_s, ag_r, c_s, c_r, y_s, y_r, x_s, x_r, k_s, k_r,
    s1_s, s1_r, fw_s, fw_r, s2_s, s2_r,
):
    width = map_ref.shape[0]
    half = width // 2
    slab = width // nz
    band, z = lax.axis_index("band"), lax.axis_index("sub")
    x, y, c = band // (2 * ny), (band // 2) % ny, band % 2

    def at(xx, yy, cc):
        return {"band": (xx * ny + yy) * 2 + cc}

    sibling = at(x, y, 1 - c)
    xpeer = {d: at((x + d) % nx, y, c) for d in range(1, nx)}
    ypeer = {d: at(x, (y + d) % ny, c) for d in range(1, ny)}
    zpeer = {d: {"sub": (z + d) % nz} for d in range(1, nz)}
    peers = [sibling, *xpeer.values(), *ypeer.values(), *zpeer.values()]
    started = []

    def send(src, dst, s, r, target):
        copy = pltpu.make_async_remote_copy(
            src_ref=src, dst_ref=dst, send_sem=s, recv_sem=r, device_id=target, device_id_type=MESH
        )
        copy.start()
        started.append(copy)
        return copy

    barrier = pltpu.get_barrier_semaphore()
    for peer in peers:
        pl.semaphore_signal(barrier, inc=1, device_id=peer, device_id_type=MESH)
    chunks = psem.shape[0]
    per = ns // chunks
    loads = []
    for q in range(chunks):
        rows = pl.ds(q * per * width, per * width)
        loads.append(pltpu.make_async_copy(panels.at[rows], pv.at[rows], psem.at[q]))
        loads[-1].start()

    def work(q):
        loads[q].wait()
        block = pv[q * per * width : (q + 1) * per * width, :]
        part = lax.dot_general(block, block, (((0,), (0,)), ((), ())), preferred_element_type=F32)
        gram[...] = part if q == 0 else gram[...] + part
        for j in range(q * per, (q + 1) * per):
            value = dot(coup_ref[j * nr : (j + 1) * nr, :], pv[j * width : (j + 1) * width, :])
            cjm[j * nr : (j + 1) * nr, :] = value
            for h in range(2):
                crm[h, pl.ds(j, nr, stride=ns), :] = value[:, h * half : (h + 1) * half]

    work(0)
    pl.semaphore_wait(barrier, len(peers))

    maps = send(map_ref, map_other, c_s.at[0], c_r.at[0], sibling)
    keys0[pl.ds(c * nx + x, 1)] = key_ref[...][None]
    keys1[pl.ds(c * ny + y, 1)] = key_ref[...][None]
    kcopies = []
    for d in range(1, nx):
        own = keys0.at[c * nx + x]
        kcopies.append(send(own, own, k_s.at[0, d], k_r.at[0, d], xpeer[d]))
    for d in range(1, ny):
        own = keys1.at[c * ny + y]
        kcopies.append(send(own, own, k_s.at[1, d], k_r.at[1, d], ypeer[d]))
    for q in range(1, chunks // 2):
        work(q)
    maps.wait_recv()
    mine, other = map_ref[...], map_other[...]
    odd = jnp.where(c == 1, mine, other)
    even = jnp.where(c == 1, other, mine)
    identity = diagonal(width).astype(F32)
    pack(product(odd, even), abuf.at[y])
    acopies = [
        send(abuf.at[y], abuf.at[y], y_s.at[0, d], y_r.at[0, d], ypeer[d]) for d in range(1, ny)
    ]
    for q in range(chunks // 2, chunks):
        work(q)

    gram[...] = gram[...] * (1.0 / (nz * ns))
    rcopies = [
        send(gram.at[pl.ds(((z + d) % nz) * slab, slab)], rsbuf.at[d], rs_s.at[d], rs_r.at[d], zpeer[d])
        for d in range(1, nz)
    ]
    for copy in kcopies:
        copy.wait_recv()
    kcopies = [
        send(keys0.at[pl.ds(c * nx, nx)], keys0.at[pl.ds(c * nx, nx)], k_s.at[0, 0], k_r.at[0, 0], sibling),
        send(keys1.at[pl.ds(c * ny, ny)], keys1.at[pl.ds(c * ny, ny)], k_s.at[1, 0], k_r.at[1, 0], sibling),
    ]
    ch, cl = split(jnp.concatenate([crm[0], crm[1]], axis=1))
    ccat[0, :, 0:width], ccat[0, :, width : 2 * width], ccat[0, :, 2 * width :] = ch, ch, cl
    ch, cl = split(cjm[...])
    ccat[1, :, 0:width], ccat[1, :, width : 2 * width], ccat[1, :, 2 * width :] = ch, ch, cl
    own = pl.ds(pl.multiple_of(z * slab, slab), slab)
    total = gram[own, :]
    for d in range(1, nz):
        rcopies[d - 1].wait_recv()
        total = total + rsbuf[d]
    upd[own, :] = total
    gcopies = [send(upd.at[own], upd.at[own], ag_s.at[d], ag_r.at[d], zpeer[d]) for d in range(1, nz)]

    def fill(cat, index, value):
        high, low = split(value)
        base = index * 3 * width
        cat[:, base : base + width] = high
        cat[:, base + width : base + 2 * width] = high
        cat[:, base + 2 * width : base + 3 * width] = low

    def conjugate(cat, buffer, count):
        for m in range(count):
            high, low = split(unpack(buffer.at[m]))
            base = m * 3 * width
            value = dot(cat[:, base : base + 3 * width], jnp.concatenate([high, low, high], axis=0))
            high, low = split(value)
            ycat[:, base : base + width] = high
            ycat[:, base + width : base + 2 * width] = low
            ycat[:, base + 2 * width : base + 3 * width] = high
        span = count * 3 * width
        return dot_t(ycat[:, 0:span], cat[:, 0:span])

    for copy in gcopies:
        copy.wait_recv()
    ucopy = send(upd, upd_other, c_s.at[1], c_r.at[1], sibling)
    for copy in acopies:
        copy.wait_recv()
    group = [unpack(abuf.at[m]) for m in range(ny)]
    running = group[ny - 1]
    for m in range(ny - 2, -1, -1):
        fill(tcat, m, running)
        running = product(running, group[m])
    pack(running, bbuf.at[x])
    bcopies = [
        send(bbuf.at[x], bbuf.at[x], x_s.at[0, d], x_r.at[0, d], xpeer[d]) for d in range(1, nx)
    ]
    ucopy.wait_recv()
    mine, other = upd[...], upd_other[...]
    upd_odd = jnp.where(c == 1, mine, other)
    upd_even = jnp.where(c == 1, other, mine)
    pack(upd_odd + dot_t_full(product(odd, upd_even), odd), vbuf.at[y])
    vcopies = [
        send(vbuf.at[y], vbuf.at[y], y_s.at[1, d], y_r.at[1, d], ypeer[d]) for d in range(1, ny)
    ]
    running = jnp.where(c == 1, even, identity)
    for m in range(ny - 2, -1, -1):
        fill(kcat, m, jnp.where(m < y, running, 0.0))
        running = product(running, jnp.where(m < y, group[m], identity))
    to_band = running

    for copy in vcopies:
        copy.wait_recv()
    pack(unpack(vbuf.at[ny - 1]) + conjugate(tcat, vbuf, ny - 1), tbuf.at[x])
    tcopies = [
        send(tbuf.at[x], tbuf.at[x], x_s.at[1, d], x_r.at[1, d], xpeer[d]) for d in range(1, nx)
    ]
    front_ref[...] = jnp.where(c == 1, upd_even, 0.0) + conjugate(kcat, vbuf, ny - 1)
    for copy in bcopies:
        copy.wait_recv()
    running = to_band
    for m in range(nx - 2, -1, -1):
        fill(wcat, m, jnp.where(m < x, running, 0.0))
        if m:
            running = product(running, jnp.where(m < x, unpack(bbuf.at[m]), identity))
    for copy in tcopies:
        copy.wait_recv()
    front = front_ref[...] + conjugate(wcat, tbuf, nx - 1)
    front_ref[...] = front

    fh, fl = split(front)
    fcat[0:width, :], fcat[width : 2 * width, :], fcat[2 * width :, :] = fh, fl, fh
    sent = dot(ccat[0], fcat[...]).astype(BF16)
    p0, p1 = c * nx + x, c * ny + y
    own0 = pl.ds(pl.multiple_of(p0 * ns, ns), ns)
    own1 = pl.ds(pl.multiple_of(p1 * ns, ns), ns)
    for r in range(nr):
        x0[own0, r * half : (r + 1) * half] = sent[r * ns : (r + 1) * ns, 0:half]
    f0 = {d: send(x0.at[own0], x0.at[own0], s1_s.at[0, d], s1_r.at[0, d], xpeer[d]) for d in range(1, nx)}
    for r in range(nr):
        x1[own1, r * half : (r + 1) * half] = sent[r * ns : (r + 1) * ns, half:]
    f1 = {d: send(x1.at[own1], x1.at[own1], s1_s.at[1, d], s1_r.at[1, d], ypeer[d]) for d in range(1, ny)}
    forwards = [
        send(x0.at[own0], x0.at[own0], fw_s.at[0, 0], fw_r.at[0, 0], sibling),
        send(x1.at[own1], x1.at[own1], fw_s.at[1, 0], fw_r.at[1, 0], sibling),
    ]
    adjoint = dot(ccat[1], fcat[...])
    for h in range(2):
        gacc[h] = adjoint[:, h * half : (h + 1) * half]
    for copy in kcopies:
        copy.wait_recv()

    def selection(keys, count, bands):
        rows, lanes = count * ns, 2 * count * ns
        lane = lax.broadcasted_iota(jnp.int32, (keys.shape[1], lanes), 1) // ns
        merged = jnp.zeros((keys.shape[1], lanes), jnp.int32)
        for p in range(2 * count):
            merged = jnp.where(lane == p, keys[p], merged)
        row = lax.broadcasted_iota(jnp.int32, (rows, lanes), 0)
        wanted = row % ns
        for m in range(count):
            wanted = wanted + jnp.where(row // ns == m, bands[m] * ns, 0)
        hits = jnp.zeros((rows, lanes), F32)
        for k in range(4):
            hits = hits + jnp.where(merged[k : k + 1, :] == wanted, 1.0, 0.0)
        return hits.astype(BF16)

    sel0 = selection(keys0, ny, [at(x, m, c)["band"] for m in range(ny)])
    sel1 = selection(keys1, nx, [at(m, y, c)["band"] for m in range(nx)])

    for d in (1, 3, 2):
        if d < nx:
            f0[d].wait_recv()
            rows = pl.ds(pl.multiple_of((c * nx + (x + nx - d) % nx) * ns, ns), ns)
            forwards.append(send(x0.at[rows], x0.at[rows], fw_s.at[0, d], fw_r.at[0, d], sibling))
        if d < ny:
            f1[d].wait_recv()
            rows = pl.ds(pl.multiple_of((c * ny + (y + ny - d) % ny) * ns, ns), ns)
            forwards.append(send(x1.at[rows], x1.at[rows], fw_s.at[1, d], fw_r.at[1, d], sibling))
    for copy in forwards:
        copy.wait_recv()
    lanes = nr * half
    for q in range(lanes // width):
        span = slice(q * width, (q + 1) * width)
        o0[:, span] = dot(sel0, x0[:, span]).astype(BF16)
    last = []
    for d in range(1, ny):
        rows = pl.ds(pl.multiple_of(((y + d) % ny) * ns, ns), ns)
        last.append(send(o0.at[rows], rb0.at[d], s2_s.at[0, d], s2_r.at[0, d], ypeer[d]))
    for q in range(lanes // width):
        span = slice(q * width, (q + 1) * width)
        o1[:, span] = dot(sel1, x1[:, span]).astype(BF16)
    for d in range(1, nx):
        rows = pl.ds(pl.multiple_of(((x + d) % nx) * ns, ns), ns)
        last.append(send(o1.at[rows], rb1.at[d], s2_s.at[1, d], s2_r.at[1, d], xpeer[d]))
    for copy in last:
        copy.wait_recv()
    home0 = o0[pl.ds(pl.multiple_of(y * ns, ns), ns), :].astype(F32)
    for d in range(1, ny):
        home0 = home0 + rb0[d].astype(F32)
    home1 = o1[pl.ds(pl.multiple_of(x * ns, ns), ns), :].astype(F32)
    for d in range(1, nx):
        home1 = home1 + rb1[d].astype(F32)
    for h, home in ((0, home0), (1, home1)):
        for r in range(nr):
            place = (h, pl.ds(r, ns, stride=nr), slice(None))
            gacc[place] = gacc[place] + home[:, r * half : (r + 1) * half]
        grads_ref[:, h * half : (h + 1) * half] = gacc[h]
    for copy in started:
        copy.wait_send()


def dot_t_full(a, b):
    ah, al = split(a)
    bh, bl = split(b)
    return dot_t(ah, bh) + (dot_t(ah, bl) + dot_t(al, bh))


def body(nx, ny, panels, chain_map, couplers, anc_band, anc_slot):
    ns, width = panels.shape[2], panels.shape[3]
    nr = couplers.shape[3]
    nz = lax.axis_size("sub")
    listed = anc_band.shape[1]
    half = width // 2
    keys = (anc_band * ns + anc_slot).T
    keys = jnp.pad(keys, ((0, 8 - listed), (0, 0)), constant_values=-1)
    sources = 2 * max(nx, ny)
    keys = jnp.tile(keys, (1, sources))
    msg = (width + PAD, width)
    dma = pltpu.SemaphoreType.DMA
    scratch = [
        pltpu.VMEM((ns * width, width), BF16),
        pltpu.VMEM((width, width), F32),
        pltpu.VMEM((nz, width // nz, width), F32),
        pltpu.VMEM((width, width), F32),
        pltpu.VMEM((width, width), F32),
        pltpu.VMEM((width, width), F32),
        pltpu.VMEM((ny, *msg), BF16),
        pltpu.VMEM((nx, *msg), BF16),
        pltpu.VMEM((ny, *msg), BF16),
        pltpu.VMEM((nx, *msg), BF16),
        pltpu.VMEM((width, 3 * width * (ny - 1)), BF16),
        pltpu.VMEM((width, 3 * width * (ny - 1)), BF16),
        pltpu.VMEM((width, 3 * width * (nx - 1)), BF16),
        pltpu.VMEM((width, 3 * width * (max(nx, ny) - 1)), BF16),
        pltpu.VMEM((2, nr * ns, half), F32),
        pltpu.VMEM((nr * ns, width), F32),
        pltpu.VMEM((2, nr * ns, half), F32),
        pltpu.VMEM((2, nr * ns, 3 * width), BF16),
        pltpu.VMEM((3 * width, width), BF16),
        pltpu.VMEM((2 * nx, 8, keys.shape[1]), jnp.int32),
        pltpu.VMEM((2 * ny, 8, keys.shape[1]), jnp.int32),
        pltpu.VMEM((2 * nx * ns, nr * half), BF16),
        pltpu.VMEM((2 * ny * ns, nr * half), BF16),
        pltpu.VMEM((ny * ns, nr * half), BF16),
        pltpu.VMEM((nx * ns, nr * half), BF16),
        pltpu.VMEM((ny, ns, nr * half), BF16),
        pltpu.VMEM((nx, ns, nr * half), BF16),
        dma((8,)),
        dma((nz,)), dma((nz,)), dma((nz,)), dma((nz,)),
        dma((2,)), dma((2,)),
        dma((2, ny)), dma((2, ny)), dma((2, nx)), dma((2, nx)),
        dma((2, 4)), dma((2, 4)),
        dma((2, 4)), dma((2, 4)), dma((2, 4)), dma((2, 4)), dma((2, 4)), dma((2, 4)),
    ]
    vmem = pl.BlockSpec(memory_space=pltpu.VMEM)
    front, grads = pl.pallas_call(
        functools.partial(kernel, nx, ny, nz, ns, nr),
        out_shape=(
            jax.ShapeDtypeStruct((width, width), F32),
            jax.ShapeDtypeStruct((ns * nr, width), F32),
        ),
        in_specs=[pl.BlockSpec(memory_space=pl.ANY), vmem, vmem, vmem],
        out_specs=(vmem, vmem),
        scratch_shapes=scratch,
        compiler_params=pltpu.CompilerParams(
            collective_id=0, has_side_effects=True, vmem_limit_bytes=48 * 2**20
        ),
        name="chain",
    )(
        panels.reshape(ns * width, width),
        chain_map[0],
        couplers.reshape(ns * nr, width),
        keys,
    )
    return front[None], grads.reshape(1, 1, ns, nr, width)


def solution(mesh, nx=CHIPS_X, ny=CHIPS_Y):
    in_specs = (
        P("band", "sub", None, None, None),
        P("band", None, None),
        P("band", "sub", None, None, None),
        P(("band", "sub"), None),
        P(("band", "sub"), None),
    )
    out_specs = (P("band", None, None), P("band", "sub", None, None, None))
    return jax.shard_map(
        functools.partial(body, nx, ny), mesh=mesh, in_specs=in_specs, out_specs=out_specs, check_vma=False
    )
```

```python
import functools

import jax
import jax.numpy as jnp
from jax import lax
from jax.experimental import pallas as pl
from jax.experimental.pallas import tpu as pltpu
from jax.sharding import PartitionSpec as P

MESH = pl.DeviceIdType.MESH
F32, BF16 = jnp.float32, jnp.bfloat16
CHIPS_X, CHIPS_Y = 4, 4
PAD = 16
CHUNKS = 2


def split(value):
    high = value.astype(BF16)
    return high, (value - high.astype(F32)).astype(BF16)


def dot(a, b):
    return jnp.dot(a, b, preferred_element_type=F32)


def dot_t(a, b):
    return lax.dot_general(a, b, (((1,), (1,)), ((), ())), preferred_element_type=F32)


def product(a, b):
    ah, al = split(a)
    bh, bl = split(b)
    return dot(ah, bh) + (dot(ah, bl) + dot(al, bh))


def product_t(a, b):
    ah, al = split(a)
    bh, bl = split(b)
    return dot_t(ah, bh) + (dot_t(ah, bl) + dot_t(al, bh))


def grid(shape, axis):
    return lax.broadcasted_iota(jnp.int32, shape, axis)


def diagonal(width):
    return grid((width, width), 0) == grid((width, width), 1)


def pick(block):
    return jnp.sum(jnp.where(diagonal(block.shape[0]), block, 0.0), axis=0, keepdims=True)


def pack_map(value, message):
    width = value.shape[1]
    high = value.astype(BF16)
    rest = pick(value - high.astype(F32))
    message[0:width, :] = high
    message[width : width + PAD, :] = jnp.broadcast_to(rest, (PAD, width)).astype(BF16)


def unpack_map(message):
    width = message.shape[1]
    rest = message[width : width + PAD, :].astype(F32)[0:1, :]
    return message[0:width, :].astype(F32) + jnp.where(diagonal(width), rest, 0.0)


def halves(full):
    half = full.shape[0] // 2
    upper = grid((half, half), 0) <= grid((half, half), 1)
    low = full[half:, half:]
    return full[:half, half:], jnp.where(upper, full[:half, :half], low), pick(low)


def halves_of_sum(full):
    half = full.shape[0] // 2
    rows, cols = grid((half, half), 0), grid((half, half), 1)
    first, low = full[:half, :half], full[half:, half:]
    side = full[:half, half:] + full[half:, :half].T
    mixed = jnp.where(rows <= cols, first, low) + jnp.where(rows >= cols, first, low).T
    return side, mixed, 2.0 * pick(low)


def one_sided(side, mixed, last):
    half = side.shape[0]
    rows, cols = grid((half, half), 0), grid((half, half), 1)
    middle = rows == cols
    first = jnp.where(rows < cols, mixed, jnp.where(middle, 0.5 * mixed, 0.0))
    low = jnp.where(rows > cols, mixed, jnp.where(middle, 0.5 * last, 0.0))
    top = jnp.concatenate([first, side], axis=1)
    return jnp.concatenate([top, jnp.concatenate([jnp.zeros_like(side), low], axis=1)], axis=0)


def pack(parts, message):
    side, mixed, last = parts
    half = side.shape[0]
    message[0:half, 0:half] = side.astype(BF16)
    high = mixed.astype(BF16)
    message[0:half, half:] = high
    rest = pick(mixed - high.astype(F32))
    last_high = last.astype(BF16).astype(F32)
    row = grid((PAD, half), 0)
    message[half : half + PAD, 0:half] = jnp.where(row == 0, rest, 0.0).astype(BF16)
    tail = jnp.where(row == 0, last - last_high, jnp.where(row == 1, last_high, 0.0))
    message[half : half + PAD, half:] = tail.astype(BF16)


def unpack(message):
    half = message.shape[1] // 2
    tail = message[half : half + PAD, :].astype(F32)
    rest = tail[0:1, 0:half]
    mixed = message[0:half, half:].astype(F32) + jnp.where(diagonal(half), rest, 0.0)
    return message[0:half, 0:half].astype(F32), mixed, tail[0:1, half:] + tail[1:2, half:]


def kernel(
    nx, ny, nz, ns, nr,
    panels, map_hbm, coup_hbm, key_hbm,
    front_ref, grads_ref,
    pv, map_ref, coup_ref, key_ref, gram, ends, rsbuf, upd, upd_other, map_other, abuf, bbuf, vbuf, tbuf,
    tcat, kcat, wcat, ycat, own_front, crm, cjm, gacc, ccat, fcat,
    keys0, keys1, xs0, xs1, x0, x1, sel0, sel1, o0, o1, rb0, rb1,
    psem, isem, rs_s, rs_r, dg_s, dg_r, ag_s, ag_r, c_s, c_r, y_s, y_r, x_s, x_r, k_s, k_r,
    s1_s, s1_r, s2_s, s2_r,
):
    width = map_ref.shape[0]
    half = width // 2
    slab = half // nz
    band, z = lax.axis_index("band"), lax.axis_index("sub")
    x, y, c = band // (2 * ny), (band // 2) % ny, band % 2

    def at(xx, yy, cc):
        return {"band": (xx * ny + yy) * 2 + cc}

    cores = (c, 1 - c)
    sibling = at(x, y, 1 - c)
    xpeer = {(d, e): at((x + d) % nx, y, cores[e]) for d in range(1, nx) for e in range(2)}
    ypeer = {(d, e): at(x, (y + d) % ny, cores[e]) for d in range(1, ny) for e in range(2)}
    zpeer = {d: {"sub": (z + d) % nz} for d in range(1, nz)}
    peers = [sibling, *xpeer.values(), *ypeer.values(), *zpeer.values()]
    started = []

    def send(src, dst, s, r, target):
        copy = pltpu.make_async_remote_copy(
            src_ref=src, dst_ref=dst, send_sem=s, recv_sem=r, device_id=target, device_id_type=MESH
        )
        copy.start()
        started.append(copy)
        return copy

    barrier = pltpu.get_barrier_semaphore()
    for peer in peers:
        pl.semaphore_signal(barrier, inc=1, device_id=peer, device_id_type=MESH)
    chunks = psem.shape[0]
    per = ns // chunks
    loads = []
    for q in range(chunks):
        rows = pl.ds(q * per * width, per * width)
        loads.append(pltpu.make_async_copy(panels.at[rows], pv.at[rows], psem.at[q]))
        loads[-1].start()
        if q == 0:
            inputs = []
            for n, (src, dst) in enumerate(((coup_hbm, coup_ref), (map_hbm, map_ref), (key_hbm, key_ref))):
                inputs.append(pltpu.make_async_copy(src, dst, isem.at[n]))
                inputs[-1].start()
    inputs[0].wait()
    for q in range(chunks):
        loads[q].wait()
        block = pv[q * per * width : (q + 1) * per * width, :]
        part = dot(block.T, block)
        gram[...] = part if q == 0 else gram[...] + part
        for j in range(q * per, (q + 1) * per):
            value = dot(coup_ref[j * nr : (j + 1) * nr, :], pv[j * width : (j + 1) * width, :])
            cjm[j * nr : (j + 1) * nr, :] = value
            for h in range(2):
                crm[h, pl.ds(j, nr, stride=ns), :] = value[:, h * half : (h + 1) * half]
    side, mixed, last = halves(gram[...] * (1.0 / (nz * ns)))
    gram[0:half, 0:half] = side
    gram[0:half, half:] = mixed
    ends[pl.ds(z, 1)] = jnp.broadcast_to(last, (8, half))[None]
    inputs[1].wait()
    inputs[2].wait()
    pl.semaphore_wait(barrier, len(peers))

    rcopies = [
        send(gram.at[pl.ds(((z + d) % nz) * slab, slab)], rsbuf.at[d], rs_s.at[d], rs_r.at[d], zpeer[d])
        for d in range(1, nz)
    ]
    maps = send(map_ref, map_other, c_s.at[0], c_r.at[0], sibling)
    dcopies = [send(ends.at[z], ends.at[z], dg_s.at[d], dg_r.at[d], zpeer[d]) for d in range(1, nz)]
    p0, p1 = c * nx + x, c * ny + y
    keys0[pl.ds(p0, 1)] = key_ref[...][None]
    keys1[pl.ds(p1, 1)] = key_ref[...][None]
    own = keys0.at[p0]
    kcopies = [send(own, own, k_s.at[0, 0, 1], k_r.at[0, 0, 1], sibling)]
    for (d, e), peer in xpeer.items():
        kcopies.append(send(own, own, k_s.at[0, d, e], k_r.at[0, d, e], peer))
    own = keys1.at[p1]
    kcopies.append(send(own, own, k_s.at[1, 0, 1], k_r.at[1, 0, 1], sibling))
    for (d, e), peer in ypeer.items():
        kcopies.append(send(own, own, k_s.at[1, d, e], k_r.at[1, d, e], peer))
    maps.wait_recv()
    mine, other = map_ref[...], map_other[...]
    odd = jnp.where(c == 1, mine, other)
    even = jnp.where(c == 1, other, mine)
    identity = diagonal(width).astype(F32)
    pack_map(product(odd, even), abuf.at[y])
    acopies = [
        send(abuf.at[y], abuf.at[y], y_s.at[0, d], y_r.at[0, d], ypeer[d, 0]) for d in range(1, ny)
    ]
    ch, cl = split(jnp.concatenate([crm[0], crm[1]], axis=1))
    ccat[0, :, 0:width], ccat[0, :, width : 2 * width], ccat[0, :, 2 * width :] = ch, ch, cl
    ch, cl = split(cjm[...])
    ccat[1, :, 0:width], ccat[1, :, width : 2 * width], ccat[1, :, 2 * width :] = ch, ch, cl
    own = pl.ds(pl.multiple_of(z * slab, slab), slab)
    total = gram[own, :]
    for d in range(1, nz):
        rcopies[d - 1].wait_recv()
        total = total + rsbuf[d]
    upd[own, :] = total
    gcopies = [send(upd.at[own], upd.at[own], ag_s.at[d], ag_r.at[d], zpeer[d]) for d in range(1, nz)]
    for copy in dcopies:
        copy.wait_recv()
    last = ends[0]
    for m in range(1, nz):
        last = last + ends[m]
    upd[half : half + 8, 0:half] = last
    upd[half : half + 8, half:] = jnp.zeros_like(last)

    def fill(cat, index, value):
        high, low = split(value)
        base = index * 3 * width
        cat[:, base : base + width] = high
        cat[:, base + width : base + 2 * width] = high
        cat[:, base + 2 * width : base + 3 * width] = low

    def conjugate(cat, buffer, count):
        for m in range(count):
            high, low = split(one_sided(*unpack(buffer.at[m])))
            base = m * 3 * width
            value = dot(cat[:, base : base + 3 * width], jnp.concatenate([high, low, high], axis=0))
            high, low = split(value)
            ycat[:, base : base + width] = high
            ycat[:, base + width : base + 2 * width] = low
            ycat[:, base + 2 * width : base + 3 * width] = high
        span = count * 3 * width
        return dot_t(ycat[:, 0:span], cat[:, 0:span])

    for copy in acopies:
        copy.wait_recv()
    group = [unpack_map(abuf.at[m]) for m in range(ny)]
    running = group[ny - 1]
    for m in range(ny - 2, -1, -1):
        fill(tcat, m, running)
        running = product(running, group[m])
    pack_map(running, bbuf.at[x])
    bcopies = [
        send(bbuf.at[x], bbuf.at[x], x_s.at[0, d], x_r.at[0, d], xpeer[d, 0]) for d in range(1, nx)
    ]
    for copy in gcopies:
        copy.wait_recv()
    ucopy = send(upd, upd_other, c_s.at[1], c_r.at[1], sibling)
    ucopy.wait_recv()
    mine, other = upd[...], upd_other[...]
    upd_odd = jnp.where(c == 1, mine, other)
    upd_even = jnp.where(c == 1, other, mine)
    upd_even = one_sided(upd_even[0:half, 0:half], upd_even[0:half, half:], upd_even[half : half + 1, 0:half])
    side, mixed, last = halves_of_sum(product_t(product(odd, upd_even), odd))
    side, mixed = side + upd_odd[0:half, 0:half], mixed + upd_odd[0:half, half:]
    pack((side, mixed, last + upd_odd[half : half + 1, 0:half]), vbuf.at[y])
    vcopies = [
        send(vbuf.at[y], vbuf.at[y], y_s.at[1, d], y_r.at[1, d], ypeer[d, 0]) for d in range(1, ny)
    ]
    running = jnp.where(c == 1, even, identity)
    for m in range(ny - 2, -1, -1):
        fill(kcat, m, jnp.where(m < y, running, 0.0))
        running = product(running, jnp.where(m < y, group[m], identity))
    to_band = running

    for copy in vcopies:
        copy.wait_recv()
    side, mixed, last = unpack(vbuf.at[ny - 1])
    more_side, more_mixed, more_last = halves_of_sum(conjugate(tcat, vbuf, ny - 1))
    pack((side + more_side, mixed + more_mixed, last + more_last), tbuf.at[x])
    tcopies = [
        send(tbuf.at[x], tbuf.at[x], x_s.at[1, d], x_r.at[1, d], xpeer[d, 0]) for d in range(1, nx)
    ]
    own_front[...] = jnp.where(c == 1, upd_even, 0.0) + conjugate(kcat, vbuf, ny - 1)
    for copy in bcopies:
        copy.wait_recv()
    running = to_band
    for m in range(nx - 2, -1, -1):
        fill(wcat, m, jnp.where(m < x, running, 0.0))
        if m:
            running = product(running, jnp.where(m < x, unpack_map(bbuf.at[m]), identity))
    for copy in kcopies:
        copy.wait_recv()

    def selection(keys, count, band_of):
        rows, lanes = 2 * count * ns, 2 * count * ns
        lane = grid((8, lanes), 1) // ns
        merged = jnp.zeros((8, lanes), jnp.int32)
        for p in range(2 * count):
            merged = jnp.where(lane == p, keys[p, :, 0:lanes], merged)
        row = grid((rows, lanes), 0)
        wanted = row % ns
        for p in range(2 * count):
            target = band_of(p % count, p // count)["band"]
            wanted = wanted + jnp.where(row // ns == p, target * ns, 0)
        hits = jnp.zeros((rows, lanes), F32)
        for k in range(4):
            hits = hits + jnp.where(merged[k : k + 1, :] == wanted, 1.0, 0.0)
        return hits.astype(BF16)

    sel0[...] = selection(keys0, ny, lambda m, core: at(x, m, core))
    sel1[...] = selection(keys1, nx, lambda m, core: at(m, y, core))
    for copy in tcopies:
        copy.wait_recv()
    front = own_front[...] + conjugate(wcat, tbuf, nx - 1)
    front = front + front.T
    front_ref[...] = front

    fh, fl = split(front)
    fcat[0:width, :], fcat[width : 2 * width, :], fcat[2 * width :, :] = fh, fl, fh
    lanes = nr * half // 2
    piece = lanes // CHUNKS
    own0 = pl.ds(pl.multiple_of(p0 * ns, ns), ns)
    own1 = pl.ds(pl.multiple_of(p1 * ns, ns), ns)
    gathers = []
    for q in range(CHUNKS):
        span = pl.ds(q * piece, piece)
        for core in range(2):
            first = (core * CHUNKS + q) * (nr // 2 // CHUNKS)
            count = nr // 2 // CHUNKS
            sent = dot(ccat[0, first * ns : (first + count) * ns, :], fcat[...]).astype(BF16)
            for r in range(count):
                place = slice(q * piece + r * half, q * piece + (r + 1) * half)
                xs0[core, :, place] = sent[r * ns : (r + 1) * ns, 0:half]
                xs1[core, :, place] = sent[r * ns : (r + 1) * ns, half:]
        batch = {}
        for h, xs, xx, rows, all_peers in ((0, xs0, x0, own0, xpeer), (1, xs1, x1, own1, ypeer)):
            batch[h] = []
            targets = {**all_peers, (0, 1): sibling}
            for (d, e), peer in targets.items():
                batch[h].append(
                    send(
                        xs.at[cores[e], :, span], xx.at[rows, span],
                        s1_s.at[q, h, d, e], s1_r.at[q, h, d, e], peer,
                    )
                )
            xx[rows, span] = xs[c, :, span]
        gathers.append(batch)
    adjoint = dot(ccat[1], fcat[...])
    for h in range(2):
        gacc[h] = adjoint[:, h * half : (h + 1) * half]
    scatters = []
    for q in range(CHUNKS):
        for h, sel, xx, oo, rb, count, all_peers in (
            (0, sel0, x0, o0, rb0, ny, ypeer), (1, sel1, x1, o1, rb1, nx, xpeer),
        ):
            here = (y, x)[h]
            for copy in gathers[q][h]:
                copy.wait_recv()
            for first in range(q * piece, (q + 1) * piece, width):
                span = slice(first, first + width)
                oo[:, span] = dot(sel[...], xx[:, span]).astype(BF16)
            span = pl.ds(q * piece, piece)
            for (d, e), peer in {**all_peers, (0, 1): sibling}.items():
                rows = pl.ds(pl.multiple_of((cores[e] * count + (here + d) % count) * ns, ns), ns)
                scatters.append(
                    send(
                        oo.at[rows, span], rb.at[d, e, :, span],
                        s2_s.at[q, h, d, e], s2_r.at[q, h, d, e], peer,
                    )
                )
    for copy in scatters:
        copy.wait_recv()
    for h, oo, rb, count, here in ((0, o0, rb0, ny, y), (1, o1, rb1, nx, x)):
        rows = pl.ds(pl.multiple_of((c * count + here) * ns, ns), ns)
        same, cross = oo[rows, :].astype(F32), rb[0, 1].astype(F32)
        for d in range(1, count):
            same, cross = same + rb[d, 0].astype(F32), cross + rb[d, 1].astype(F32)
        parts = jnp.where(c == 0, same, cross), jnp.where(c == 0, cross, same)
        for r in range(nr):
            place = (h, pl.ds(r, ns, stride=nr), slice(None))
            lane = r % (nr // 2) * half
            gacc[place] = gacc[place] + parts[r // (nr // 2)][:, lane : lane + half]
        grads_ref[:, h * half : (h + 1) * half] = gacc[h]
    for copy in started:
        copy.wait_send()


def body(nx, ny, panels, chain_map, couplers, anc_band, anc_slot):
    ns, width = panels.shape[2], panels.shape[3]
    nr = couplers.shape[3]
    nz = lax.axis_size("sub")
    listed = anc_band.shape[1]
    half = width // 2
    keys = (anc_band * ns + anc_slot).T
    keys = jnp.pad(keys, ((0, 8 - listed), (0, 0)), constant_values=-1)
    keys = jnp.tile(keys, (1, 2 * max(nx, ny)))
    lanes = nr * half // 2
    mapmsg, symmsg = (width + PAD, width), (half + PAD, width)
    far = max(nx, ny)
    dma = lambda *shape: pltpu.SemaphoreType.DMA(shape)
    scratch = [
        pltpu.VMEM((ns * width, width), BF16),
        pltpu.VMEM((width, width), F32),
        pltpu.VMEM((nr * ns, width), BF16),
        pltpu.VMEM(keys.shape, jnp.int32),
        pltpu.VMEM((width, width), F32),
        pltpu.VMEM((nz, 8, half), F32),
        pltpu.VMEM((nz, half // nz, width), F32),
        pltpu.VMEM((half + 8, width), F32),
        pltpu.VMEM((half + 8, width), F32),
        pltpu.VMEM((width, width), F32),
        pltpu.VMEM((ny, *mapmsg), BF16),
        pltpu.VMEM((nx, *mapmsg), BF16),
        pltpu.VMEM((ny, *symmsg), BF16),
        pltpu.VMEM((nx, *symmsg), BF16),
        pltpu.VMEM((width, 3 * width * (ny - 1)), BF16),
        pltpu.VMEM((width, 3 * width * (ny - 1)), BF16),
        pltpu.VMEM((width, 3 * width * (nx - 1)), BF16),
        pltpu.VMEM((width, 3 * width * (far - 1)), BF16),
        pltpu.VMEM((width, width), F32),
        pltpu.VMEM((2, nr * ns, half), F32),
        pltpu.VMEM((nr * ns, width), F32),
        pltpu.VMEM((2, nr * ns, half), F32),
        pltpu.VMEM((2, nr * ns, 3 * width), BF16),
        pltpu.VMEM((3 * width, width), BF16),
        pltpu.VMEM((2 * nx, *keys.shape), jnp.int32),
        pltpu.VMEM((2 * ny, *keys.shape), jnp.int32),
        pltpu.VMEM((2, ns, lanes), BF16),
        pltpu.VMEM((2, ns, lanes), BF16),
        pltpu.VMEM((2 * nx * ns, lanes), BF16),
        pltpu.VMEM((2 * ny * ns, lanes), BF16),
        pltpu.VMEM((2 * ny * ns, 2 * ny * ns), BF16),
        pltpu.VMEM((2 * nx * ns, 2 * nx * ns), BF16),
        pltpu.VMEM((2 * ny * ns, lanes), BF16),
        pltpu.VMEM((2 * nx * ns, lanes), BF16),
        pltpu.VMEM((ny, 2, ns, lanes), BF16),
        pltpu.VMEM((nx, 2, ns, lanes), BF16),
        dma(8), dma(3),
        dma(nz), dma(nz), dma(nz), dma(nz), dma(nz), dma(nz),
        dma(2), dma(2),
        dma(2, ny), dma(2, ny), dma(2, nx), dma(2, nx),
        dma(2, far, 2), dma(2, far, 2),
        dma(CHUNKS, 2, far, 2), dma(CHUNKS, 2, far, 2), dma(CHUNKS, 2, far, 2), dma(CHUNKS, 2, far, 2),
    ]
    vmem = pl.BlockSpec(memory_space=pltpu.VMEM)
    hbm = pl.BlockSpec(memory_space=pl.ANY)
    front, grads = pl.pallas_call(
        functools.partial(kernel, nx, ny, nz, ns, nr),
        out_shape=(
            jax.ShapeDtypeStruct((width, width), F32),
            jax.ShapeDtypeStruct((ns * nr, width), F32),
        ),
        in_specs=[hbm] * 4,
        out_specs=(vmem, vmem),
        scratch_shapes=scratch,
        compiler_params=pltpu.CompilerParams(
            collective_id=0, has_side_effects=True, vmem_limit_bytes=56 * 2**20
        ),
        name="chain",
    )(
        panels.reshape(ns * width, width),
        chain_map[0],
        couplers.reshape(ns * nr, width),
        keys,
    )
    return front[None], grads.reshape(1, 1, ns, nr, width)


def solution(mesh, nx=CHIPS_X, ny=CHIPS_Y):
    in_specs = (
        P("band", "sub", None, None, None),
        P("band", None, None),
        P("band", "sub", None, None, None),
        P(("band", "sub"), None),
        P(("band", "sub"), None),
    )
    out_specs = (P("band", None, None), P("band", "sub", None, None, None))
    return jax.shard_map(
        functools.partial(body, nx, ny), mesh=mesh, in_specs=in_specs, out_specs=out_specs, check_vma=False
    )
```

```python
import functools

import jax
import jax.numpy as jnp
from jax import lax
from jax.experimental import pallas as pl
from jax.experimental.pallas import tpu as pltpu
from jax.sharding import PartitionSpec as P

MESH = pl.DeviceIdType.MESH
F32, BF16 = jnp.float32, jnp.bfloat16
CHIPS_X, CHIPS_Y = 4, 4
PAD = 16
CHUNKS = 2


def split(value):
    high = value.astype(BF16)
    return high, (value - high.astype(F32)).astype(BF16)


def dot(a, b):
    return jnp.dot(a, b, preferred_element_type=F32)


def dot_t(a, b):
    return lax.dot_general(a, b, (((1,), (1,)), ((), ())), preferred_element_type=F32)


def product(a, b):
    ah, al = split(a)
    bh, bl = split(b)
    return dot(ah, bh) + (dot(ah, bl) + dot(al, bh))


def product_t(a, b):
    ah, al = split(a)
    bh, bl = split(b)
    return dot_t(ah, bh) + (dot_t(ah, bl) + dot_t(al, bh))


def grid(shape, axis):
    return lax.broadcasted_iota(jnp.int32, shape, axis)


def diagonal(width):
    return grid((width, width), 0) == grid((width, width), 1)


def pick(block):
    return jnp.sum(jnp.where(diagonal(block.shape[0]), block, 0.0), axis=0, keepdims=True)


def pack_map(value, message):
    width = value.shape[1]
    high = value.astype(BF16)
    rest = pick(value - high.astype(F32))
    message[0:width, :] = high
    message[width : width + PAD, :] = jnp.broadcast_to(rest, (PAD, width)).astype(BF16)


def unpack_map(message):
    width = message.shape[1]
    rest = message[width : width + PAD, :].astype(F32)[0:1, :]
    return message[0:width, :].astype(F32) + jnp.where(diagonal(width), rest, 0.0)


def halves(full):
    half = full.shape[0] // 2
    upper = grid((half, half), 0) <= grid((half, half), 1)
    low = full[half:, half:]
    return full[:half, half:], jnp.where(upper, full[:half, :half], low), pick(low)


def halves_of_sum(full):
    half = full.shape[0] // 2
    rows, cols = grid((half, half), 0), grid((half, half), 1)
    first, low = full[:half, :half], full[half:, half:]
    side = full[:half, half:] + full[half:, :half].T
    mixed = jnp.where(rows <= cols, first, low) + jnp.where(rows >= cols, first, low).T
    return side, mixed, 2.0 * pick(low)


def one_sided(side, mixed, last):
    half = side.shape[0]
    rows, cols = grid((half, half), 0), grid((half, half), 1)
    middle = rows == cols
    first = jnp.where(rows < cols, mixed, jnp.where(middle, 0.5 * mixed, 0.0))
    low = jnp.where(rows > cols, mixed, jnp.where(middle, 0.5 * last, 0.0))
    top = jnp.concatenate([first, side], axis=1)
    return jnp.concatenate([top, jnp.concatenate([jnp.zeros_like(side), low], axis=1)], axis=0)


def pack(parts, message):
    side, mixed, last = parts
    half = side.shape[0]
    message[0:half, 0:half] = side.astype(BF16)
    high = mixed.astype(BF16)
    message[0:half, half:] = high
    rest = pick(mixed - high.astype(F32))
    last_high = last.astype(BF16).astype(F32)
    row = grid((PAD, half), 0)
    message[half : half + PAD, 0:half] = jnp.where(row == 0, rest, 0.0).astype(BF16)
    tail = jnp.where(row == 0, last - last_high, jnp.where(row == 1, last_high, 0.0))
    message[half : half + PAD, half:] = tail.astype(BF16)


def unpack(message):
    half = message.shape[1] // 2
    tail = message[half : half + PAD, :].astype(F32)
    rest = tail[0:1, 0:half]
    mixed = message[0:half, half:].astype(F32) + jnp.where(diagonal(half), rest, 0.0)
    return message[0:half, 0:half].astype(F32), mixed, tail[0:1, half:] + tail[1:2, half:]


def kernel(
    nx, ny, nz, ns, nr,
    panels, map_hbm, coup_hbm, band_hbm, slot_hbm,
    front_ref, grads_ref,
    pv, map_ref, coup_ref, band_ref, slot_ref, gram, ends, rsbuf, upd, upd_other, map_other, abuf, bbuf, vbuf, tbuf,
    tcat, kcat, wcat, ycat, own_front, crm, cjm, gacc, ccat, fcat,
    keys0, keys1, xs0, xs1, x0, x1, sel0, sel1, o0, o1, rb0, rb1,
    psem, isem, rs_s, rs_r, dg_s, dg_r, ag_s, ag_r, c_s, c_r, y_s, y_r, x_s, x_r, k_s, k_r,
    s1_s, s1_r, s2_s, s2_r,
):
    width = map_ref.shape[0]
    half = width // 2
    slab = half // nz
    band, z = lax.axis_index("band"), lax.axis_index("sub")
    x, y, c = band // (2 * ny), (band // 2) % ny, band % 2

    def at(xx, yy, cc):
        return {"band": (xx * ny + yy) * 2 + cc}

    cores = (c, 1 - c)
    sibling = at(x, y, 1 - c)
    xpeer = {(d, e): at((x + d) % nx, y, cores[e]) for d in range(1, nx) for e in range(2)}
    ypeer = {(d, e): at(x, (y + d) % ny, cores[e]) for d in range(1, ny) for e in range(2)}
    zpeer = {d: {"sub": (z + d) % nz} for d in range(1, nz)}
    peers = [sibling, *xpeer.values(), *ypeer.values(), *zpeer.values()]
    started = []

    def send(src, dst, s, r, target):
        copy = pltpu.make_async_remote_copy(
            src_ref=src, dst_ref=dst, send_sem=s, recv_sem=r, device_id=target, device_id_type=MESH
        )
        copy.start()
        started.append(copy)
        return copy

    barrier = pltpu.get_barrier_semaphore()
    for peer in peers:
        pl.semaphore_signal(barrier, inc=1, device_id=peer, device_id_type=MESH)
    chunks = psem.shape[0]
    per = ns // chunks
    loads = []
    for q in range(chunks):
        rows = pl.ds(q * per * width, per * width)
        loads.append(pltpu.make_async_copy(panels.at[rows], pv.at[rows], psem.at[q]))
        loads[-1].start()
        if q == 0:
            inputs = []
            small = ((coup_hbm, coup_ref), (map_hbm, map_ref), (band_hbm, band_ref), (slot_hbm, slot_ref))
            for n, (src, dst) in enumerate(small):
                inputs.append(pltpu.make_async_copy(src, dst, isem.at[n]))
                inputs[-1].start()
    inputs[0].wait()
    for q in range(chunks):
        loads[q].wait()
        block = pv[q * per * width : (q + 1) * per * width, :]
        part = dot(block.T, block)
        gram[...] = part if q == 0 else gram[...] + part
        for j in range(q * per, (q + 1) * per):
            value = dot(coup_ref[j * nr : (j + 1) * nr, :], pv[j * width : (j + 1) * width, :])
            cjm[j * nr : (j + 1) * nr, :] = value
            for h in range(2):
                crm[h, pl.ds(j, nr, stride=ns), :] = value[:, h * half : (h + 1) * half]
    side, mixed, last = halves(gram[...] * (1.0 / (nz * ns)))
    gram[0:half, 0:half] = side
    gram[0:half, half:] = mixed
    ends[pl.ds(z, 1)] = jnp.broadcast_to(last, (8, half))[None]
    for copy in inputs[1:]:
        copy.wait()
    pl.semaphore_wait(barrier, len(peers))

    rcopies = [
        send(gram.at[pl.ds(((z + d) % nz) * slab, slab)], rsbuf.at[d], rs_s.at[d], rs_r.at[d], zpeer[d])
        for d in range(1, nz)
    ]
    maps = send(map_ref, map_other, c_s.at[0], c_r.at[0], sibling)
    dcopies = [send(ends.at[z], ends.at[z], dg_s.at[d], dg_r.at[d], zpeer[d]) for d in range(1, nz)]
    p0, p1 = c * nx + x, c * ny + y
    keys = band_ref[...] * ns + slot_ref[...]
    keys = jnp.concatenate([keys, jnp.full((8 - keys.shape[0], ns), -1, jnp.int32)], axis=0)
    keys = jnp.concatenate([keys] * (keys0.shape[2] // ns), axis=1)
    keys0[pl.ds(p0, 1)] = keys[None]
    keys1[pl.ds(p1, 1)] = keys[None]
    own = keys0.at[p0]
    kcopies = [send(own, own, k_s.at[0, 0, 1], k_r.at[0, 0, 1], sibling)]
    for (d, e), peer in xpeer.items():
        kcopies.append(send(own, own, k_s.at[0, d, e], k_r.at[0, d, e], peer))
    own = keys1.at[p1]
    kcopies.append(send(own, own, k_s.at[1, 0, 1], k_r.at[1, 0, 1], sibling))
    for (d, e), peer in ypeer.items():
        kcopies.append(send(own, own, k_s.at[1, d, e], k_r.at[1, d, e], peer))
    maps.wait_recv()
    mine, other = map_ref[...], map_other[...]
    odd = jnp.where(c == 1, mine, other)
    even = jnp.where(c == 1, other, mine)
    identity = diagonal(width).astype(F32)
    pack_map(product(odd, even), abuf.at[y])
    acopies = [
        send(abuf.at[y], abuf.at[y], y_s.at[0, d], y_r.at[0, d], ypeer[d, 0]) for d in range(1, ny)
    ]
    ch, cl = split(jnp.concatenate([crm[0], crm[1]], axis=1))
    ccat[0, :, 0:width], ccat[0, :, width : 2 * width], ccat[0, :, 2 * width :] = ch, ch, cl
    ch, cl = split(cjm[...])
    ccat[1, :, 0:width], ccat[1, :, width : 2 * width], ccat[1, :, 2 * width :] = ch, ch, cl
    own = pl.ds(pl.multiple_of(z * slab, slab), slab)
    total = gram[own, :]
    for d in range(1, nz):
        rcopies[d - 1].wait_recv()
        total = total + rsbuf[d]
    upd[own, :] = total
    gcopies = [send(upd.at[own], upd.at[own], ag_s.at[d], ag_r.at[d], zpeer[d]) for d in range(1, nz)]
    for copy in dcopies:
        copy.wait_recv()
    last = ends[0]
    for m in range(1, nz):
        last = last + ends[m]
    upd[half : half + 8, 0:half] = last
    upd[half : half + 8, half:] = jnp.zeros_like(last)

    def fill(cat, index, value):
        high, low = split(value)
        base = index * 3 * width
        cat[:, base : base + width] = high
        cat[:, base + width : base + 2 * width] = high
        cat[:, base + 2 * width : base + 3 * width] = low

    def conjugate(cat, buffer, count):
        for m in range(count):
            high, low = split(one_sided(*unpack(buffer.at[m])))
            base = m * 3 * width
            value = dot(cat[:, base : base + 3 * width], jnp.concatenate([high, low, high], axis=0))
            high, low = split(value)
            ycat[:, base : base + width] = high
            ycat[:, base + width : base + 2 * width] = low
            ycat[:, base + 2 * width : base + 3 * width] = high
        span = count * 3 * width
        return dot_t(ycat[:, 0:span], cat[:, 0:span])

    for copy in gcopies:
        copy.wait_recv()
    ucopy = send(upd, upd_other, c_s.at[1], c_r.at[1], sibling)
    ucopy.wait_recv()
    mine, other = upd[...], upd_other[...]
    upd_odd = jnp.where(c == 1, mine, other)
    upd_even = jnp.where(c == 1, other, mine)
    upd_even = one_sided(upd_even[0:half, 0:half], upd_even[0:half, half:], upd_even[half : half + 1, 0:half])
    side, mixed, last = halves_of_sum(product_t(product(odd, upd_even), odd))
    side, mixed = side + upd_odd[0:half, 0:half], mixed + upd_odd[0:half, half:]
    pack((side, mixed, last + upd_odd[half : half + 1, 0:half]), vbuf.at[y])
    vcopies = [
        send(vbuf.at[y], vbuf.at[y], y_s.at[1, d], y_r.at[1, d], ypeer[d, 0]) for d in range(1, ny)
    ]
    for copy in acopies:
        copy.wait_recv()
    group = [unpack_map(abuf.at[m]) for m in range(ny)]
    running = group[ny - 1]
    for m in range(ny - 2, -1, -1):
        fill(tcat, m, running)
        running = product(running, group[m])
    pack_map(running, bbuf.at[x])
    bcopies = [
        send(bbuf.at[x], bbuf.at[x], x_s.at[0, d], x_r.at[0, d], xpeer[d, 0]) for d in range(1, nx)
    ]
    running = jnp.where(c == 1, even, identity)
    for m in range(ny - 2, -1, -1):
        fill(kcat, m, jnp.where(m < y, running, 0.0))
        running = product(running, jnp.where(m < y, group[m], identity))
    to_band = running

    for copy in vcopies:
        copy.wait_recv()
    side, mixed, last = unpack(vbuf.at[ny - 1])
    more_side, more_mixed, more_last = halves_of_sum(conjugate(tcat, vbuf, ny - 1))
    pack((side + more_side, mixed + more_mixed, last + more_last), tbuf.at[x])
    tcopies = [
        send(tbuf.at[x], tbuf.at[x], x_s.at[1, d], x_r.at[1, d], xpeer[d, 0]) for d in range(1, nx)
    ]
    own_front[...] = jnp.where(c == 1, upd_even, 0.0) + conjugate(kcat, vbuf, ny - 1)
    for copy in bcopies:
        copy.wait_recv()
    running = to_band
    for m in range(nx - 2, -1, -1):
        fill(wcat, m, jnp.where(m < x, running, 0.0))
        if m:
            running = product(running, jnp.where(m < x, unpack_map(bbuf.at[m]), identity))
    for copy in kcopies:
        copy.wait_recv()

    def selection(keys, count, band_of):
        rows, lanes = 2 * count * ns, 2 * count * ns
        lane = grid((8, lanes), 1) // ns
        merged = jnp.zeros((8, lanes), jnp.int32)
        for p in range(2 * count):
            merged = jnp.where(lane == p, keys[p, :, 0:lanes], merged)
        row = grid((rows, lanes), 0)
        wanted = row % ns
        for p in range(2 * count):
            target = band_of(p % count, p // count)["band"]
            wanted = wanted + jnp.where(row // ns == p, target * ns, 0)
        hits = jnp.zeros((rows, lanes), F32)
        for k in range(4):
            hits = hits + jnp.where(merged[k : k + 1, :] == wanted, 1.0, 0.0)
        return hits.astype(BF16)

    sel0[...] = selection(keys0, ny, lambda m, core: at(x, m, core))
    sel1[...] = selection(keys1, nx, lambda m, core: at(m, y, core))
    for copy in tcopies:
        copy.wait_recv()
    front = own_front[...] + conjugate(wcat, tbuf, nx - 1)
    front = front + front.T
    front_ref[...] = front

    fh, fl = split(front)
    fcat[0:width, :], fcat[width : 2 * width, :], fcat[2 * width :, :] = fh, fl, fh
    lanes = nr * half // 2
    piece = lanes // CHUNKS
    own0 = pl.ds(pl.multiple_of(p0 * ns, ns), ns)
    own1 = pl.ds(pl.multiple_of(p1 * ns, ns), ns)
    gathers = []
    for q in range(CHUNKS):
        span = pl.ds(q * piece, piece)
        for core in range(2):
            first = (core * CHUNKS + q) * (nr // 2 // CHUNKS)
            count = nr // 2 // CHUNKS
            sent = dot(ccat[0, first * ns : (first + count) * ns, :], fcat[...]).astype(BF16)
            for r in range(count):
                place = slice(q * piece + r * half, q * piece + (r + 1) * half)
                xs0[core, :, place] = sent[r * ns : (r + 1) * ns, 0:half]
                xs1[core, :, place] = sent[r * ns : (r + 1) * ns, half:]
        batch = {}
        for h, xs, xx, rows, all_peers in ((0, xs0, x0, own0, xpeer), (1, xs1, x1, own1, ypeer)):
            batch[h] = []
            targets = {**all_peers, (0, 1): sibling}
            for (d, e), peer in targets.items():
                batch[h].append(
                    send(
                        xs.at[cores[e], :, span], xx.at[rows, span],
                        s1_s.at[q, h, d, e], s1_r.at[q, h, d, e], peer,
                    )
                )
            xx[rows, span] = xs[c, :, span]
        gathers.append(batch)
    adjoint = dot(ccat[1], fcat[...])
    for h in range(2):
        gacc[h] = adjoint[:, h * half : (h + 1) * half]
    scatters = []
    for q in range(CHUNKS):
        for h, sel, xx, oo, rb, count, all_peers in (
            (0, sel0, x0, o0, rb0, ny, ypeer), (1, sel1, x1, o1, rb1, nx, xpeer),
        ):
            here = (y, x)[h]
            for copy in gathers[q][h]:
                copy.wait_recv()
            for first in range(q * piece, (q + 1) * piece, width):
                span = slice(first, first + width)
                oo[:, span] = dot(sel[...], xx[:, span]).astype(BF16)
            span = pl.ds(q * piece, piece)
            for (d, e), peer in {**all_peers, (0, 1): sibling}.items():
                rows = pl.ds(pl.multiple_of((cores[e] * count + (here + d) % count) * ns, ns), ns)
                scatters.append(
                    send(
                        oo.at[rows, span], rb.at[d, e, :, span],
                        s2_s.at[q, h, d, e], s2_r.at[q, h, d, e], peer,
                    )
                )
    for copy in scatters:
        copy.wait_recv()
    for h, oo, rb, count, here in ((0, o0, rb0, ny, y), (1, o1, rb1, nx, x)):
        rows = pl.ds(pl.multiple_of((c * count + here) * ns, ns), ns)
        same, cross = oo[rows, :].astype(F32), rb[0, 1].astype(F32)
        for d in range(1, count):
            same, cross = same + rb[d, 0].astype(F32), cross + rb[d, 1].astype(F32)
        parts = jnp.where(c == 0, same, cross), jnp.where(c == 0, cross, same)
        for r in range(nr):
            place = (h, pl.ds(r, ns, stride=nr), slice(None))
            lane = r % (nr // 2) * half
            gacc[place] = gacc[place] + parts[r // (nr // 2)][:, lane : lane + half]
        grads_ref[:, h * half : (h + 1) * half] = gacc[h]
    for copy in started:
        copy.wait_send()


def body(nx, ny, panels, chain_map, couplers, anc_band, anc_slot):
    ns, width = panels.shape[2], panels.shape[3]
    nr = couplers.shape[3]
    nz = lax.axis_size("sub")
    listed = anc_band.shape[1]
    half = width // 2
    sources = 2 * max(nx, ny)
    lanes = nr * half // 2
    mapmsg, symmsg = (width + PAD, width), (half + PAD, width)
    far = max(nx, ny)
    dma = lambda *shape: pltpu.SemaphoreType.DMA(shape)
    scratch = [
        pltpu.VMEM((ns * width, width), BF16),
        pltpu.VMEM((width, width), F32),
        pltpu.VMEM((nr * ns, width), BF16),
        pltpu.VMEM((listed, ns), jnp.int32),
        pltpu.VMEM((listed, ns), jnp.int32),
        pltpu.VMEM((width, width), F32),
        pltpu.VMEM((nz, 8, half), F32),
        pltpu.VMEM((nz, half // nz, width), F32),
        pltpu.VMEM((half + 8, width), F32),
        pltpu.VMEM((half + 8, width), F32),
        pltpu.VMEM((width, width), F32),
        pltpu.VMEM((ny, *mapmsg), BF16),
        pltpu.VMEM((nx, *mapmsg), BF16),
        pltpu.VMEM((ny, *symmsg), BF16),
        pltpu.VMEM((nx, *symmsg), BF16),
        pltpu.VMEM((width, 3 * width * (ny - 1)), BF16),
        pltpu.VMEM((width, 3 * width * (ny - 1)), BF16),
        pltpu.VMEM((width, 3 * width * (nx - 1)), BF16),
        pltpu.VMEM((width, 3 * width * (far - 1)), BF16),
        pltpu.VMEM((width, width), F32),
        pltpu.VMEM((2, nr * ns, half), F32),
        pltpu.VMEM((nr * ns, width), F32),
        pltpu.VMEM((2, nr * ns, half), F32),
        pltpu.VMEM((2, nr * ns, 3 * width), BF16),
        pltpu.VMEM((3 * width, width), BF16),
        pltpu.VMEM((2 * nx, 8, sources * ns), jnp.int32),
        pltpu.VMEM((2 * ny, 8, sources * ns), jnp.int32),
        pltpu.VMEM((2, ns, lanes), BF16),
        pltpu.VMEM((2, ns, lanes), BF16),
        pltpu.VMEM((2 * nx * ns, lanes), BF16),
        pltpu.VMEM((2 * ny * ns, lanes), BF16),
        pltpu.VMEM((2 * ny * ns, 2 * ny * ns), BF16),
        pltpu.VMEM((2 * nx * ns, 2 * nx * ns), BF16),
        pltpu.VMEM((2 * ny * ns, lanes), BF16),
        pltpu.VMEM((2 * nx * ns, lanes), BF16),
        pltpu.VMEM((ny, 2, ns, lanes), BF16),
        pltpu.VMEM((nx, 2, ns, lanes), BF16),
        dma(8), dma(4),
        dma(nz), dma(nz), dma(nz), dma(nz), dma(nz), dma(nz),
        dma(2), dma(2),
        dma(2, ny), dma(2, ny), dma(2, nx), dma(2, nx),
        dma(2, far, 2), dma(2, far, 2),
        dma(CHUNKS, 2, far, 2), dma(CHUNKS, 2, far, 2), dma(CHUNKS, 2, far, 2), dma(CHUNKS, 2, far, 2),
    ]
    vmem = pl.BlockSpec(memory_space=pltpu.VMEM)
    hbm = pl.BlockSpec(memory_space=pl.ANY)
    front, grads = pl.pallas_call(
        functools.partial(kernel, nx, ny, nz, ns, nr),
        out_shape=(
            jax.ShapeDtypeStruct((width, width), F32),
            jax.ShapeDtypeStruct((ns * nr, width), F32),
        ),
        in_specs=[hbm] * 5,
        out_specs=(vmem, vmem),
        scratch_shapes=scratch,
        compiler_params=pltpu.CompilerParams(
            collective_id=0, has_side_effects=True, vmem_limit_bytes=48 * 2**20
        ),
        name="chain",
    )(
        *(
            pltpu.with_memory_space_constraint(array, pltpu.HBM)
            for array in (
                panels.reshape(ns * width, width),
                chain_map[0],
                couplers.reshape(ns * nr, width),
                anc_band.T,
                anc_slot.T,
            )
        )
    )
    return front[None], grads.reshape(1, 1, ns, nr, width)


def solution(mesh, nx=CHIPS_X, ny=CHIPS_Y):
    in_specs = (
        P("band", "sub", None, None, None),
        P("band", None, None),
        P("band", "sub", None, None, None),
        P(("band", "sub"), None),
        P(("band", "sub"), None),
    )
    out_specs = (P("band", None, None), P("band", "sub", None, None, None))
    return jax.shard_map(
        functools.partial(body, nx, ny), mesh=mesh, in_specs=in_specs, out_specs=out_specs, check_vma=False
    )
```

```python
import functools

import jax
import jax.numpy as jnp
from jax import lax
from jax.experimental import pallas as pl
from jax.experimental.pallas import tpu as pltpu
from jax.sharding import PartitionSpec as P

MESH = pl.DeviceIdType.MESH
F32, BF16 = jnp.float32, jnp.bfloat16
CHIPS_X, CHIPS_Y = 4, 4
PAD = 16
CHUNKS = 2
AHEAD = 3


def split(value):
    high = value.astype(BF16)
    return high, (value - high.astype(F32)).astype(BF16)


def dot(a, b):
    return jnp.dot(a, b, preferred_element_type=F32)


def dot_t(a, b):
    return lax.dot_general(a, b, (((1,), (1,)), ((), ())), preferred_element_type=F32)


def product(a, b):
    ah, al = split(a)
    bh, bl = split(b)
    return dot(ah, bh) + (dot(ah, bl) + dot(al, bh))


def product_t(a, b):
    ah, al = split(a)
    bh, bl = split(b)
    return dot_t(ah, bh) + (dot_t(ah, bl) + dot_t(al, bh))


def grid(shape, axis):
    return lax.broadcasted_iota(jnp.int32, shape, axis)


def diagonal(width):
    return grid((width, width), 0) == grid((width, width), 1)


def pick(block):
    return jnp.sum(jnp.where(diagonal(block.shape[0]), block, 0.0), axis=0, keepdims=True)


def pack_map(value, message):
    width = value.shape[1]
    high = value.astype(BF16)
    rest = pick(value - high.astype(F32))
    message[0:width, :] = high
    message[width : width + PAD, :] = jnp.broadcast_to(rest, (PAD, width)).astype(BF16)


def unpack_map(message):
    width = message.shape[1]
    rest = message[width : width + PAD, :].astype(F32)[0:1, :]
    return message[0:width, :].astype(F32) + jnp.where(diagonal(width), rest, 0.0)


def halves(full):
    half = full.shape[0] // 2
    upper = grid((half, half), 0) <= grid((half, half), 1)
    low = full[half:, half:]
    return full[:half, half:], jnp.where(upper, full[:half, :half], low), pick(low)


def halves_of_sum(full):
    half = full.shape[0] // 2
    rows, cols = grid((half, half), 0), grid((half, half), 1)
    first, low = full[:half, :half], full[half:, half:]
    side = full[:half, half:] + full[half:, :half].T
    mixed = jnp.where(rows <= cols, first, low) + jnp.where(rows >= cols, first, low).T
    return side, mixed, 2.0 * pick(low)


def one_sided(side, mixed, last):
    half = side.shape[0]
    rows, cols = grid((half, half), 0), grid((half, half), 1)
    middle = rows == cols
    first = jnp.where(rows < cols, mixed, jnp.where(middle, 0.5 * mixed, 0.0))
    low = jnp.where(rows > cols, mixed, jnp.where(middle, 0.5 * last, 0.0))
    top = jnp.concatenate([first, side], axis=1)
    return jnp.concatenate([top, jnp.concatenate([jnp.zeros_like(side), low], axis=1)], axis=0)


def pack(parts, message):
    side, mixed, last = parts
    half = side.shape[0]
    message[0:half, 0:half] = side.astype(BF16)
    high = mixed.astype(BF16)
    message[0:half, half:] = high
    rest = pick(mixed - high.astype(F32))
    last_high = last.astype(BF16).astype(F32)
    row = grid((PAD, half), 0)
    message[half : half + PAD, 0:half] = jnp.where(row == 0, rest, 0.0).astype(BF16)
    tail = jnp.where(row == 0, last - last_high, jnp.where(row == 1, last_high, 0.0))
    message[half : half + PAD, half:] = tail.astype(BF16)


def unpack(message):
    half = message.shape[1] // 2
    tail = message[half : half + PAD, :].astype(F32)
    rest = tail[0:1, 0:half]
    mixed = message[0:half, half:].astype(F32) + jnp.where(diagonal(half), rest, 0.0)
    return message[0:half, 0:half].astype(F32), mixed, tail[0:1, half:] + tail[1:2, half:]


def far_first(count):
    return sorted(range(1, count), key=lambda d: -min(d, count - d))


def kernel(
    nx, ny, nz, ns, nr,
    panels, map_hbm, coup_hbm, band_hbm, slot_hbm,
    front_ref, grads_ref,
    pv, map_ref, coup_ref, band_ref, slot_ref, gram, ends, rsbuf, upd, upd_other, map_other, abuf, bbuf, vbuf, tbuf,
    tcat, kcat, wcat, own_front, crm, cjm, gacc, ccat, fcat,
    keys0, keys1, xs0, xs1, x0, x1, sel0, sel1, o0, o1, rb0, rb1,
    psem, isem, rs_s, rs_r, dg_s, dg_r, ag_s, ag_r, c_s, c_r, y_s, y_r, x_s, x_r, k_s, k_r,
    s1_s, s1_r, s2_s, s2_r,
):
    width = map_ref.shape[0]
    half = width // 2
    slab = half // nz
    band, z = lax.axis_index("band"), lax.axis_index("sub")
    x, y, c = band // (2 * ny), (band // 2) % ny, band % 2

    def at(xx, yy, cc):
        return {"band": (xx * ny + yy) * 2 + cc}

    cores = (c, 1 - c)
    sibling = at(x, y, 1 - c)
    xpeer = {(d, e): at((x + d) % nx, y, cores[e]) for d in far_first(nx) for e in range(2)}
    ypeer = {(d, e): at(x, (y + d) % ny, cores[e]) for d in far_first(ny) for e in range(2)}
    zpeer = {d: {"sub": (z + d) % nz} for d in far_first(nz)}
    peers = [sibling, *xpeer.values(), *ypeer.values(), *zpeer.values()]
    started = []

    def send(src, dst, s, r, target):
        copy = pltpu.make_async_remote_copy(
            src_ref=src, dst_ref=dst, send_sem=s, recv_sem=r, device_id=target, device_id_type=MESH
        )
        copy.start()
        started.append(copy)
        return copy

    barrier = pltpu.get_barrier_semaphore()
    for peer in peers:
        pl.semaphore_signal(barrier, inc=1, device_id=peer, device_id_type=MESH)
    chunks = psem.shape[0]
    per = ns // chunks
    loads = []
    for q in range(chunks):
        rows = pl.ds(q * per * width, per * width)
        loads.append(pltpu.make_async_copy(panels.at[rows], pv.at[rows], psem.at[q]))
        if q < AHEAD:
            loads[-1].start()
        if q == 0:
            inputs = []
            small = ((coup_hbm, coup_ref), (map_hbm, map_ref), (band_hbm, band_ref), (slot_hbm, slot_ref))
            for n, (src, dst) in enumerate(small):
                inputs.append(pltpu.make_async_copy(src, dst, isem.at[n]))
                inputs[-1].start()
    inputs[0].wait()
    for q in range(chunks):
        loads[q].wait()
        if q + AHEAD < chunks:
            loads[q + AHEAD].start()
        block = pv[q * per * width : (q + 1) * per * width, :]
        part = dot(block.T, block)
        gram[...] = part if q == 0 else gram[...] + part
        for j in range(q * per, (q + 1) * per):
            value = dot(coup_ref[j * nr : (j + 1) * nr, :], pv[j * width : (j + 1) * width, :])
            cjm[j * nr : (j + 1) * nr, :] = value
            for h in range(2):
                crm[h, pl.ds(j, nr, stride=ns), :] = value[:, h * half : (h + 1) * half]
    side, mixed, last = halves(gram[...] * (1.0 / (nz * ns)))
    gram[0:half, 0:half] = side
    gram[0:half, half:] = mixed
    ends[pl.ds(z, 1)] = last[None]
    for copy in inputs[1:]:
        copy.wait()
    pl.semaphore_wait(barrier, len(peers))

    rcopies = {
        d: send(gram.at[pl.ds(((z + d) % nz) * slab, slab)], rsbuf.at[d], rs_s.at[d], rs_r.at[d], peer)
        for d, peer in zpeer.items()
    }
    maps = send(map_ref, map_other, c_s.at[0], c_r.at[0], sibling)
    dcopies = [send(ends.at[z], ends.at[z], dg_s.at[d], dg_r.at[d], peer) for d, peer in zpeer.items()]
    p0, p1 = c * nx + x, c * ny + y
    keys = band_ref[...] * ns + slot_ref[...]
    keys = jnp.concatenate([keys, jnp.full((8 - keys.shape[0], ns), -1, jnp.int32)], axis=0)
    keys = jnp.concatenate([keys] * (keys0.shape[2] // ns), axis=1)
    keys0[pl.ds(p0, 1)] = keys[None]
    keys1[pl.ds(p1, 1)] = keys[None]
    own = keys0.at[p0]
    kcopies = [send(own, own, k_s.at[0, 0, 1], k_r.at[0, 0, 1], sibling)]
    for (d, e), peer in xpeer.items():
        kcopies.append(send(own, own, k_s.at[0, d, e], k_r.at[0, d, e], peer))
    own = keys1.at[p1]
    kcopies.append(send(own, own, k_s.at[1, 0, 1], k_r.at[1, 0, 1], sibling))
    for (d, e), peer in ypeer.items():
        kcopies.append(send(own, own, k_s.at[1, d, e], k_r.at[1, d, e], peer))
    maps.wait_recv()
    mine, other = map_ref[...], map_other[...]
    odd = jnp.where(c == 1, mine, other)
    even = jnp.where(c == 1, other, mine)
    identity = diagonal(width).astype(F32)
    pack_map(product(odd, even), abuf.at[y])
    acopies = [send(abuf.at[y], abuf.at[y], y_s.at[0, d], y_r.at[0, d], ypeer[d, 0]) for d in far_first(ny)]
    ch, cl = split(jnp.concatenate([crm[0], crm[1]], axis=1))
    ccat[0, :, 0:width], ccat[0, :, width : 2 * width], ccat[0, :, 2 * width :] = ch, ch, cl
    ch, cl = split(cjm[...])
    ccat[1, :, 0:width], ccat[1, :, width : 2 * width], ccat[1, :, 2 * width :] = ch, ch, cl
    own = pl.ds(pl.multiple_of(z * slab, slab), slab)
    total = gram[own, :]
    for d in range(1, nz):
        rcopies[d].wait_recv()
        total = total + rsbuf[d]
    upd[own, :] = total
    gcopies = [send(upd.at[own], upd.at[own], ag_s.at[d], ag_r.at[d], peer) for d, peer in zpeer.items()]
    for copy in dcopies:
        copy.wait_recv()
    last = ends[0]
    for m in range(1, nz):
        last = last + ends[m]
    last = jnp.broadcast_to(last, (8, half))
    upd[half : half + 8, 0:half] = last
    upd[half : half + 8, half:] = jnp.zeros_like(last)

    def fill(cat, index, value):
        high, low = split(value)
        cat[index, :, 0:width] = high
        cat[index, :, width : 2 * width] = high
        cat[index, :, 2 * width :] = low

    def term(cat, buffer, m):
        high, low = split(one_sided(*unpack(buffer.at[m])))
        spread = cat[m]
        high, low = split(dot(spread, jnp.concatenate([high, low, high], axis=0)))
        return dot_t(jnp.concatenate([high, low, high], axis=1), spread)

    for copy in gcopies:
        copy.wait_recv()
    ucopy = send(upd, upd_other, c_s.at[1], c_r.at[1], sibling)
    ucopy.wait_recv()
    mine, other = upd[...], upd_other[...]
    upd_odd = jnp.where(c == 1, mine, other)
    upd_even = jnp.where(c == 1, other, mine)
    upd_even = one_sided(upd_even[0:half, 0:half], upd_even[0:half, half:], upd_even[half : half + 1, 0:half])
    side, mixed, last = halves_of_sum(product_t(product(odd, upd_even), odd))
    side, mixed = side + upd_odd[0:half, 0:half], mixed + upd_odd[0:half, half:]
    pack((side, mixed, last + upd_odd[half : half + 1, 0:half]), vbuf.at[y])
    vcopies = {
        d: send(vbuf.at[y], vbuf.at[y], y_s.at[1, d], y_r.at[1, d], ypeer[d, 0]) for d in far_first(ny)
    }
    for copy in acopies:
        copy.wait_recv()
    group = [unpack_map(abuf.at[m]) for m in range(ny)]
    fill(tcat, ny - 1, identity)
    running = group[ny - 1]
    for m in range(ny - 2, -1, -1):
        fill(tcat, m, running)
        running = product(running, group[m])
    pack_map(running, bbuf.at[x])
    bcopies = [send(bbuf.at[x], bbuf.at[x], x_s.at[0, d], x_r.at[0, d], xpeer[d, 0]) for d in far_first(nx)]
    running = jnp.where(c == 1, even, identity)
    for m in range(ny - 2, -1, -1):
        fill(kcat, m, jnp.where(m < y, running, 0.0))
        running = product(running, jnp.where(m < y, group[m], identity))
    to_band = running
    fill(kcat, ny - 1, jnp.zeros_like(running))

    total = term(tcat, vbuf, y)
    for d in reversed(far_first(ny)):
        vcopies[d].wait_recv()
        total = total + term(tcat, vbuf, (y + ny - d) % ny)
    pack(halves_of_sum(total), tbuf.at[x])
    tcopies = {
        d: send(tbuf.at[x], tbuf.at[x], x_s.at[1, d], x_r.at[1, d], xpeer[d, 0]) for d in far_first(nx)
    }
    total = jnp.where(c == 1, upd_even, 0.0)
    for d in range(1, ny):
        total = total + term(kcat, vbuf, (y + ny - d) % ny)
    own_front[...] = total
    for copy in bcopies:
        copy.wait_recv()
    running = to_band
    fill(wcat, nx - 1, jnp.zeros_like(running))
    for m in range(nx - 2, -1, -1):
        fill(wcat, m, jnp.where(m < x, running, 0.0))
        if m:
            running = product(running, jnp.where(m < x, unpack_map(bbuf.at[m]), identity))
    for copy in kcopies:
        copy.wait_recv()

    def selection(keys, count, band_of):
        rows, lanes = 2 * count * ns, 2 * count * ns
        lane = grid((8, lanes), 1) // ns
        merged = jnp.zeros((8, lanes), jnp.int32)
        for p in range(2 * count):
            merged = jnp.where(lane == p, keys[p, :, 0:lanes], merged)
        row = grid((rows, lanes), 0)
        wanted = row % ns
        for p in range(2 * count):
            target = band_of(p % count, p // count)["band"]
            wanted = wanted + jnp.where(row // ns == p, target * ns, 0)
        hits = jnp.zeros((rows, lanes), F32)
        for k in range(4):
            hits = hits + jnp.where(merged[k : k + 1, :] == wanted, 1.0, 0.0)
        return hits.astype(BF16)

    sel0[...] = selection(keys0, ny, lambda m, core: at(x, m, core))
    sel1[...] = selection(keys1, nx, lambda m, core: at(m, y, core))
    front = own_front[...]
    for d in reversed(far_first(nx)):
        tcopies[d].wait_recv()
        front = front + term(wcat, tbuf, (x + nx - d) % nx)
    front = front + front.T
    front_ref[...] = front

    fh, fl = split(front)
    fcat[0:width, :], fcat[width : 2 * width, :], fcat[2 * width :, :] = fh, fl, fh
    lanes = nr * half // 2
    piece = lanes // CHUNKS
    own0 = pl.ds(pl.multiple_of(p0 * ns, ns), ns)
    own1 = pl.ds(pl.multiple_of(p1 * ns, ns), ns)
    gathers = []
    for q in range(CHUNKS):
        span = pl.ds(q * piece, piece)
        for core in range(2):
            first = (core * CHUNKS + q) * (nr // 2 // CHUNKS)
            count = nr // 2 // CHUNKS
            sent = dot(ccat[0, first * ns : (first + count) * ns, :], fcat[...]).astype(BF16)
            for r in range(count):
                place = slice(q * piece + r * half, q * piece + (r + 1) * half)
                xs0[core, :, place] = sent[r * ns : (r + 1) * ns, 0:half]
                xs1[core, :, place] = sent[r * ns : (r + 1) * ns, half:]
        batch = {}
        for h, xs, xx, rows, all_peers in ((0, xs0, x0, own0, xpeer), (1, xs1, x1, own1, ypeer)):
            batch[h] = []
            targets = {**all_peers, (0, 1): sibling}
            for (d, e), peer in targets.items():
                batch[h].append(
                    send(
                        xs.at[cores[e], :, span], xx.at[rows, span],
                        s1_s.at[q, h, d, e], s1_r.at[q, h, d, e], peer,
                    )
                )
            xx[rows, span] = xs[c, :, span]
        gathers.append(batch)
    adjoint = dot(ccat[1], fcat[...])
    for h in range(2):
        gacc[h] = adjoint[:, h * half : (h + 1) * half]
    scatters = []
    for q in range(CHUNKS):
        for h, sel, xx, oo, rb, count, all_peers in (
            (0, sel0, x0, o0, rb0, ny, ypeer), (1, sel1, x1, o1, rb1, nx, xpeer),
        ):
            here = (y, x)[h]
            for copy in gathers[q][h]:
                copy.wait_recv()
            for first in range(q * piece, (q + 1) * piece, width):
                span = slice(first, first + width)
                oo[:, span] = dot(sel[...], xx[:, span]).astype(BF16)
            span = pl.ds(q * piece, piece)
            for (d, e), peer in {**all_peers, (0, 1): sibling}.items():
                rows = pl.ds(pl.multiple_of((cores[e] * count + (here + d) % count) * ns, ns), ns)
                scatters.append(
                    send(
                        oo.at[rows, span], rb.at[d, e, :, span],
                        s2_s.at[q, h, d, e], s2_r.at[q, h, d, e], peer,
                    )
                )
    for copy in scatters:
        copy.wait_recv()
    for h, oo, rb, count, here in ((0, o0, rb0, ny, y), (1, o1, rb1, nx, x)):
        rows = pl.ds(pl.multiple_of((c * count + here) * ns, ns), ns)
        same, cross = oo[rows, :].astype(F32), rb[0, 1].astype(F32)
        for d in range(1, count):
            same, cross = same + rb[d, 0].astype(F32), cross + rb[d, 1].astype(F32)
        parts = jnp.where(c == 0, same, cross), jnp.where(c == 0, cross, same)
        for r in range(nr):
            place = (h, pl.ds(r, ns, stride=nr), slice(None))
            lane = r % (nr // 2) * half
            gacc[place] = gacc[place] + parts[r // (nr // 2)][:, lane : lane + half]
        grads_ref[:, h * half : (h + 1) * half] = gacc[h]
    for copy in started:
        copy.wait_send()


def body(nx, ny, panels, chain_map, couplers, anc_band, anc_slot):
    ns, width = panels.shape[2], panels.shape[3]
    nr = couplers.shape[3]
    nz = lax.axis_size("sub")
    listed = anc_band.shape[1]
    half = width // 2
    sources = 2 * max(nx, ny)
    lanes = nr * half // 2
    mapmsg, symmsg = (width + PAD, width), (half + PAD, width)
    far = max(nx, ny)
    dma = lambda *shape: pltpu.SemaphoreType.DMA(shape)
    scratch = [
        pltpu.VMEM((ns * width, width), BF16),
        pltpu.VMEM((width, width), F32),
        pltpu.VMEM((nr * ns, width), BF16),
        pltpu.VMEM((listed, ns), jnp.int32),
        pltpu.VMEM((listed, ns), jnp.int32),
        pltpu.VMEM((width, width), F32),
        pltpu.VMEM((nz, 1, half), F32),
        pltpu.VMEM((nz, half // nz, width), F32),
        pltpu.VMEM((half + 8, width), F32),
        pltpu.VMEM((half + 8, width), F32),
        pltpu.VMEM((width, width), F32),
        pltpu.VMEM((ny, *mapmsg), BF16),
        pltpu.VMEM((nx, *mapmsg), BF16),
        pltpu.VMEM((ny, *symmsg), BF16),
        pltpu.VMEM((nx, *symmsg), BF16),
        pltpu.VMEM((ny, width, 3 * width), BF16),
        pltpu.VMEM((ny, width, 3 * width), BF16),
        pltpu.VMEM((nx, width, 3 * width), BF16),
        pltpu.VMEM((width, width), F32),
        pltpu.VMEM((2, nr * ns, half), F32),
        pltpu.VMEM((nr * ns, width), F32),
        pltpu.VMEM((2, nr * ns, half), F32),
        pltpu.VMEM((2, nr * ns, 3 * width), BF16),
        pltpu.VMEM((3 * width, width), BF16),
        pltpu.VMEM((2 * nx, 8, sources * ns), jnp.int32),
        pltpu.VMEM((2 * ny, 8, sources * ns), jnp.int32),
        pltpu.VMEM((2, ns, lanes), BF16),
        pltpu.VMEM((2, ns, lanes), BF16),
        pltpu.VMEM((2 * nx * ns, lanes), BF16),
        pltpu.VMEM((2 * ny * ns, lanes), BF16),
        pltpu.VMEM((2 * ny * ns, 2 * ny * ns), BF16),
        pltpu.VMEM((2 * nx * ns, 2 * nx * ns), BF16),
        pltpu.VMEM((2 * ny * ns, lanes), BF16),
        pltpu.VMEM((2 * nx * ns, lanes), BF16),
        pltpu.VMEM((ny, 2, ns, lanes), BF16),
        pltpu.VMEM((nx, 2, ns, lanes), BF16),
        dma(8), dma(4),
        dma(nz), dma(nz), dma(nz), dma(nz), dma(nz), dma(nz),
        dma(2), dma(2),
        dma(2, ny), dma(2, ny), dma(2, nx), dma(2, nx),
        dma(2, far, 2), dma(2, far, 2),
        dma(CHUNKS, 2, far, 2), dma(CHUNKS, 2, far, 2), dma(CHUNKS, 2, far, 2), dma(CHUNKS, 2, far, 2),
    ]
    vmem = pl.BlockSpec(memory_space=pltpu.VMEM)
    hbm = pl.BlockSpec(memory_space=pl.ANY)
    front, grads = pl.pallas_call(
        functools.partial(kernel, nx, ny, nz, ns, nr),
        out_shape=(
            jax.ShapeDtypeStruct((width, width), F32),
            jax.ShapeDtypeStruct((ns * nr, width), F32),
        ),
        in_specs=[hbm] * 5,
        out_specs=(vmem, vmem),
        scratch_shapes=scratch,
        compiler_params=pltpu.CompilerParams(
            collective_id=0, has_side_effects=True, vmem_limit_bytes=48 * 2**20
        ),
        name="chain",
    )(
        *(
            pltpu.with_memory_space_constraint(array, pltpu.HBM)
            for array in (
                panels.reshape(ns * width, width),
                chain_map[0],
                couplers.reshape(ns * nr, width),
                anc_band.T,
                anc_slot.T,
            )
        )
    )
    return front[None], grads.reshape(1, 1, ns, nr, width)


def solution(mesh, nx=CHIPS_X, ny=CHIPS_Y):
    in_specs = (
        P("band", "sub", None, None, None),
        P("band", None, None),
        P("band", "sub", None, None, None),
        P(("band", "sub"), None),
        P(("band", "sub"), None),
    )
    out_specs = (P("band", None, None), P("band", "sub", None, None, None))
    return jax.shard_map(
        functools.partial(body, nx, ny), mesh=mesh, in_specs=in_specs, out_specs=out_specs, check_vma=False
    )
```

```python
import functools

import jax
import jax.numpy as jnp
from jax import lax
from jax.experimental import pallas as pl
from jax.experimental.pallas import tpu as pltpu
from jax.sharding import PartitionSpec as P

MESH = pl.DeviceIdType.MESH
F32, BF16 = jnp.float32, jnp.bfloat16
CHIPS_X, CHIPS_Y = 4, 4
PAD = 16
CHUNKS = 2
AHEAD = 3


def split(value):
    high = value.astype(BF16)
    return high, (value - high.astype(F32)).astype(BF16)


def dot(a, b):
    return jnp.dot(a, b, preferred_element_type=F32)


def dot_t(a, b):
    return lax.dot_general(a, b, (((1,), (1,)), ((), ())), preferred_element_type=F32)


def product(a, b):
    ah, al = split(a)
    bh, bl = split(b)
    return dot(ah, bh) + (dot(ah, bl) + dot(al, bh))


def product_t(a, b):
    ah, al = split(a)
    bh, bl = split(b)
    return dot_t(ah, bh) + (dot_t(ah, bl) + dot_t(al, bh))


def grid(shape, axis):
    return lax.broadcasted_iota(jnp.int32, shape, axis)


def diagonal(width):
    return grid((width, width), 0) == grid((width, width), 1)


def pick(block):
    return jnp.sum(jnp.where(diagonal(block.shape[0]), block, 0.0), axis=0, keepdims=True)


def pack_map(value, message):
    width = value.shape[1]
    high = value.astype(BF16)
    rest = pick(value - high.astype(F32))
    message[0:width, :] = high
    message[width : width + PAD, :] = jnp.broadcast_to(rest, (PAD, width)).astype(BF16)


def unpack_map(message):
    width = message.shape[1]
    rest = message[width : width + PAD, :].astype(F32)[0:1, :]
    return message[0:width, :].astype(F32) + jnp.where(diagonal(width), rest, 0.0)


def halves(full):
    half = full.shape[0] // 2
    upper = grid((half, half), 0) <= grid((half, half), 1)
    low = full[half:, half:]
    return full[:half, half:], jnp.where(upper, full[:half, :half], low), pick(low)


def halves_of_sum(full):
    half = full.shape[0] // 2
    rows, cols = grid((half, half), 0), grid((half, half), 1)
    first, low = full[:half, :half], full[half:, half:]
    side = full[:half, half:] + full[half:, :half].T
    mixed = jnp.where(rows <= cols, first, low) + jnp.where(rows >= cols, first, low).T
    return side, mixed, 2.0 * pick(low)


def one_sided(side, mixed, last):
    half = side.shape[0]
    rows, cols = grid((half, half), 0), grid((half, half), 1)
    middle = rows == cols
    first = jnp.where(rows < cols, mixed, jnp.where(middle, 0.5 * mixed, 0.0))
    low = jnp.where(rows > cols, mixed, jnp.where(middle, 0.5 * last, 0.0))
    top = jnp.concatenate([first, side], axis=1)
    return jnp.concatenate([top, jnp.concatenate([jnp.zeros_like(side), low], axis=1)], axis=0)


def parts_of(rows):
    half = rows.shape[1] // 2
    mixed = jnp.where(diagonal(half), rows[half : half + 1, 0:half], rows[0:half, half:])
    return rows[0:half, 0:half], mixed, rows[half : half + 1, half:]


def pack(parts, message):
    side, mixed, last = parts
    half = side.shape[0]
    message[0:half, 0:half] = side.astype(BF16)
    high = mixed.astype(BF16)
    message[0:half, half:] = high
    rest = pick(mixed - high.astype(F32))
    last_high = last.astype(BF16).astype(F32)
    row = grid((PAD, half), 0)
    message[half : half + PAD, 0:half] = jnp.where(row == 0, rest, 0.0).astype(BF16)
    tail = jnp.where(row == 0, last - last_high, jnp.where(row == 1, last_high, 0.0))
    message[half : half + PAD, half:] = tail.astype(BF16)


def unpack(message):
    half = message.shape[1] // 2
    tail = message[half : half + PAD, :].astype(F32)
    rest = tail[0:1, 0:half]
    mixed = message[0:half, half:].astype(F32) + jnp.where(diagonal(half), rest, 0.0)
    return message[0:half, 0:half].astype(F32), mixed, tail[0:1, half:] + tail[1:2, half:]


def far_first(count):
    return sorted(range(1, count), key=lambda d: -min(d, count - d))


def kernel(
    nx, ny, nz, ns, nr,
    panels, map_hbm, coup_hbm, band_hbm, slot_hbm,
    front_ref, grads_ref,
    pv, map_ref, coup_ref, band_ref, slot_ref, gram, shares, ends, rsbuf, upd, upd_other, map_other, abuf, bbuf, vbuf, tbuf,
    tcat, kcat, wcat, own_front, crm, cjm, gacc, ccat, fcat,
    keys0, keys1, xs0, xs1, x0, x1, sel0, sel1, o0, o1, rb0, rb1,
    psem, isem, rs_s, rs_r, dg_s, dg_r, ag_s, ag_r, c_s, c_r, y_s, y_r, x_s, x_r, k_s, k_r,
    s1_s, s1_r, s2_s, s2_r,
):
    width = map_ref.shape[0]
    half = width // 2
    slab = half // nz
    band, z = lax.axis_index("band"), lax.axis_index("sub")
    x, y, c = band // (2 * ny), (band // 2) % ny, band % 2

    def at(xx, yy, cc):
        return {"band": (xx * ny + yy) * 2 + cc}

    cores = (c, 1 - c)
    sibling = at(x, y, 1 - c)
    xpeer = {(d, e): at((x + d) % nx, y, cores[e]) for d in far_first(nx) for e in range(2)}
    ypeer = {(d, e): at(x, (y + d) % ny, cores[e]) for d in far_first(ny) for e in range(2)}
    zpeer = {d: {"sub": (z + d) % nz} for d in far_first(nz)}
    peers = [*zpeer.values(), *xpeer.values(), *ypeer.values(), sibling]
    started = []

    def send(src, dst, s, r, target):
        copy = pltpu.make_async_remote_copy(
            src_ref=src, dst_ref=dst, send_sem=s, recv_sem=r, device_id=target, device_id_type=MESH
        )
        copy.start()
        started.append(copy)
        return copy

    barrier = pltpu.get_barrier_semaphore()
    for peer in peers:
        pl.semaphore_signal(barrier, inc=1, device_id=peer, device_id_type=MESH)
    chunks = psem.shape[0]
    per = ns // chunks
    loads = []
    for q in range(chunks):
        rows = pl.ds(q * per * width, per * width)
        loads.append(pltpu.make_async_copy(panels.at[rows], pv.at[rows], psem.at[q]))
        if q < AHEAD:
            loads[-1].start()
        if q == 0:
            inputs = []
            small = ((coup_hbm, coup_ref), (map_hbm, map_ref), (band_hbm, band_ref), (slot_hbm, slot_ref))
            for n, (src, dst) in enumerate(small):
                inputs.append(pltpu.make_async_copy(src, dst, isem.at[n]))
                inputs[-1].start()
    inputs[0].wait()
    for q in range(chunks):
        loads[q].wait()
        if q + AHEAD < chunks:
            loads[q + AHEAD].start()
        block = pv[q * per * width : (q + 1) * per * width, :]
        part = dot(block.T, block)
        gram[...] = part if q == 0 else gram[...] + part
        for j in range(q * per, (q + 1) * per):
            value = dot(coup_ref[j * nr : (j + 1) * nr, :], pv[j * width : (j + 1) * width, :])
            cjm[j * nr : (j + 1) * nr, :] = value
            for h in range(2):
                crm[h, pl.ds(j, nr, stride=ns), :] = value[:, h * half : (h + 1) * half]
    side, mixed, last = halves(gram[...] * (1.0 / (nz * ns)))
    packed = jnp.concatenate([side, mixed], axis=1)
    gram[0:half, :] = packed
    shares[...] = packed.astype(BF16)
    ends[pl.ds(z, 1)] = jnp.concatenate([pick(mixed), last], axis=1)[None]
    for copy in inputs[1:]:
        copy.wait()
    pl.semaphore_wait(barrier, len(peers))

    rcopies = {
        d: send(shares.at[pl.ds(((z + d) % nz) * slab, slab)], rsbuf.at[d], rs_s.at[d], rs_r.at[d], peer)
        for d, peer in zpeer.items()
    }
    maps = send(map_ref, map_other, c_s.at[0], c_r.at[0], sibling)
    dcopies = [send(ends.at[z], ends.at[z], dg_s.at[d], dg_r.at[d], peer) for d, peer in zpeer.items()]
    p0, p1 = c * nx + x, c * ny + y
    keys = band_ref[...] * ns + slot_ref[...]
    keys = jnp.concatenate([keys, jnp.full((8 - keys.shape[0], ns), -1, jnp.int32)], axis=0)
    keys = jnp.concatenate([keys] * (keys0.shape[2] // ns), axis=1)
    keys0[pl.ds(p0, 1)] = keys[None]
    keys1[pl.ds(p1, 1)] = keys[None]
    own = keys0.at[p0]
    kcopies = [send(own, own, k_s.at[0, 0, 1], k_r.at[0, 0, 1], sibling)]
    for (d, e), peer in xpeer.items():
        kcopies.append(send(own, own, k_s.at[0, d, e], k_r.at[0, d, e], peer))
    own = keys1.at[p1]
    kcopies.append(send(own, own, k_s.at[1, 0, 1], k_r.at[1, 0, 1], sibling))
    for (d, e), peer in ypeer.items():
        kcopies.append(send(own, own, k_s.at[1, d, e], k_r.at[1, d, e], peer))
    maps.wait_recv()
    mine, other = map_ref[...], map_other[...]
    odd = jnp.where(c == 1, mine, other)
    even = jnp.where(c == 1, other, mine)
    identity = diagonal(width).astype(F32)
    pack_map(product(odd, even), abuf.at[y])
    acopies = [send(abuf.at[y], abuf.at[y], y_s.at[0, d], y_r.at[0, d], ypeer[d, 0]) for d in far_first(ny)]
    ch, cl = split(jnp.concatenate([crm[0], crm[1]], axis=1))
    ccat[0, :, 0:width], ccat[0, :, width : 2 * width], ccat[0, :, 2 * width :] = ch, ch, cl
    ch, cl = split(cjm[...])
    ccat[1, :, 0:width], ccat[1, :, width : 2 * width], ccat[1, :, 2 * width :] = ch, ch, cl
    own = pl.ds(pl.multiple_of(z * slab, slab), slab)
    total = gram[own, :]
    for d in range(1, nz):
        rcopies[d].wait_recv()
        total = total + rsbuf[d].astype(F32)
    upd[own, :] = total
    gcopies = [send(upd.at[own], upd.at[own], ag_s.at[d], ag_r.at[d], peer) for d, peer in zpeer.items()]
    for copy in dcopies:
        copy.wait_recv()
    last = ends[0]
    for m in range(1, nz):
        last = last + ends[m]
    upd[half : half + 8, :] = jnp.broadcast_to(last, (8, width))

    def fill(cat, index, value):
        high, low = split(value)
        cat[index, :, 0:width] = high
        cat[index, :, width : 2 * width] = high
        cat[index, :, 2 * width :] = low

    def term(cat, buffer, m):
        high, low = split(one_sided(*unpack(buffer.at[m])))
        spread = cat[m]
        high, low = split(dot(spread, jnp.concatenate([high, low, high], axis=0)))
        return dot_t(jnp.concatenate([high, low, high], axis=1), spread)

    for copy in gcopies:
        copy.wait_recv()
    ucopy = send(upd, upd_other, c_s.at[1], c_r.at[1], sibling)
    ucopy.wait_recv()
    mine, other = upd[...], upd_other[...]
    upd_odd = jnp.where(c == 1, mine, other)
    upd_even = jnp.where(c == 1, other, mine)
    upd_even = one_sided(*parts_of(upd_even))
    side, mixed, last = halves_of_sum(product_t(product(odd, upd_even), odd))
    more = parts_of(upd_odd)
    pack((side + more[0], mixed + more[1], last + more[2]), vbuf.at[y])
    vcopies = {
        d: send(vbuf.at[y], vbuf.at[y], y_s.at[1, d], y_r.at[1, d], ypeer[d, 0]) for d in far_first(ny)
    }
    for copy in acopies:
        copy.wait_recv()
    group = [unpack_map(abuf.at[m]) for m in range(ny)]
    fill(tcat, ny - 1, identity)
    running = group[ny - 1]
    for m in range(ny - 2, -1, -1):
        fill(tcat, m, running)
        running = product(running, group[m])
    pack_map(running, bbuf.at[x])
    bcopies = [send(bbuf.at[x], bbuf.at[x], x_s.at[0, d], x_r.at[0, d], xpeer[d, 0]) for d in far_first(nx)]
    running = jnp.where(c == 1, even, identity)
    for m in range(ny - 2, -1, -1):
        fill(kcat, m, jnp.where(m < y, running, 0.0))
        running = product(running, jnp.where(m < y, group[m], identity))
    to_band = running
    fill(kcat, ny - 1, jnp.zeros_like(running))

    total = term(tcat, vbuf, y)
    for d in reversed(far_first(ny)):
        vcopies[d].wait_recv()
        total = total + term(tcat, vbuf, (y + ny - d) % ny)
    pack(halves_of_sum(total), tbuf.at[x])
    tcopies = {
        d: send(tbuf.at[x], tbuf.at[x], x_s.at[1, d], x_r.at[1, d], xpeer[d, 0]) for d in far_first(nx)
    }
    total = jnp.where(c == 1, upd_even, 0.0)
    for d in range(1, ny):
        total = total + term(kcat, vbuf, (y + ny - d) % ny)
    own_front[...] = total
    for copy in bcopies:
        copy.wait_recv()
    running = to_band
    fill(wcat, nx - 1, jnp.zeros_like(running))
    for m in range(nx - 2, -1, -1):
        fill(wcat, m, jnp.where(m < x, running, 0.0))
        if m:
            running = product(running, jnp.where(m < x, unpack_map(bbuf.at[m]), identity))
    for copy in kcopies:
        copy.wait_recv()

    def selection(keys, count, band_of):
        rows, lanes = 2 * count * ns, 2 * count * ns
        lane = grid((8, lanes), 1) // ns
        merged = jnp.zeros((8, lanes), jnp.int32)
        for p in range(2 * count):
            merged = jnp.where(lane == p, keys[p, :, 0:lanes], merged)
        row = grid((rows, lanes), 0)
        wanted = row % ns
        for p in range(2 * count):
            target = band_of(p % count, p // count)["band"]
            wanted = wanted + jnp.where(row // ns == p, target * ns, 0)
        hits = jnp.zeros((rows, lanes), F32)
        for k in range(4):
            hits = hits + jnp.where(merged[k : k + 1, :] == wanted, 1.0, 0.0)
        return hits.astype(BF16)

    sel0[...] = selection(keys0, ny, lambda m, core: at(x, m, core))
    sel1[...] = selection(keys1, nx, lambda m, core: at(m, y, core))
    front = own_front[...]
    for copy in tcopies.values():
        copy.wait_recv()
    for d in range(1, nx):
        front = front + term(wcat, tbuf, (x + nx - d) % nx)
    front = front + front.T
    front_ref[...] = front

    fh, fl = split(front)
    fcat[0:width, :], fcat[width : 2 * width, :], fcat[2 * width :, :] = fh, fl, fh
    lanes = nr * half // 2
    piece = lanes // CHUNKS
    own0 = pl.ds(pl.multiple_of(p0 * ns, ns), ns)
    own1 = pl.ds(pl.multiple_of(p1 * ns, ns), ns)
    gathers = []
    for q in range(CHUNKS):
        span = pl.ds(q * piece, piece)
        for core in range(2):
            first = (core * CHUNKS + q) * (nr // 2 // CHUNKS)
            count = nr // 2 // CHUNKS
            sent = dot(ccat[0, first * ns : (first + count) * ns, :], fcat[...]).astype(BF16)
            for r in range(count):
                place = slice(q * piece + r * half, q * piece + (r + 1) * half)
                xs0[core, :, place] = sent[r * ns : (r + 1) * ns, 0:half]
                xs1[core, :, place] = sent[r * ns : (r + 1) * ns, half:]
        batch = {}
        for h, xs, xx, rows, all_peers in ((0, xs0, x0, own0, xpeer), (1, xs1, x1, own1, ypeer)):
            batch[h] = []
            targets = {**all_peers, (0, 1): sibling}
            for (d, e), peer in targets.items():
                batch[h].append(
                    send(
                        xs.at[cores[e], :, span], xx.at[rows, span],
                        s1_s.at[q, h, d, e], s1_r.at[q, h, d, e], peer,
                    )
                )
            xx[rows, span] = xs[c, :, span]
        gathers.append(batch)
    adjoint = dot(ccat[1], fcat[...])
    for h in range(2):
        gacc[h] = adjoint[:, h * half : (h + 1) * half]
    scatters = {}
    for q in range(CHUNKS):
        for h, sel, xx, oo, rb, count, all_peers in (
            (0, sel0, x0, o0, rb0, ny, ypeer), (1, sel1, x1, o1, rb1, nx, xpeer),
        ):
            here = (y, x)[h]
            for copy in gathers[q][h]:
                copy.wait_recv()
            for first in range(q * piece, (q + 1) * piece, width):
                span = slice(first, first + width)
                oo[:, span] = dot(sel[...], xx[:, span]).astype(BF16)
            span = pl.ds(q * piece, piece)
            scatters[q, h] = []
            for (d, e), peer in {**all_peers, (0, 1): sibling}.items():
                rows = pl.ds(pl.multiple_of((cores[e] * count + (here + d) % count) * ns, ns), ns)
                scatters[q, h].append(
                    send(
                        oo.at[rows, span], rb.at[d, e, :, span],
                        s2_s.at[q, h, d, e], s2_r.at[q, h, d, e], peer,
                    )
                )
    for q in range(CHUNKS):
        for h, oo, rb, count, here in ((0, o0, rb0, ny, y), (1, o1, rb1, nx, x)):
            for copy in scatters[q, h]:
                copy.wait_recv()
            span = pl.ds(q * piece, piece)
            rows = pl.ds(pl.multiple_of((c * count + here) * ns, ns), ns)
            same, cross = oo[rows, span].astype(F32), rb[0, 1, :, span].astype(F32)
            for d in range(1, count):
                same, cross = same + rb[d, 0, :, span].astype(F32), cross + rb[d, 1, :, span].astype(F32)
            for core, part in enumerate((jnp.where(c == 0, same, cross), jnp.where(c == 0, cross, same))):
                for r in range(piece // half):
                    place = (h, pl.ds((core * CHUNKS + q) * (piece // half) + r, ns, stride=nr), slice(None))
                    gacc[place] = gacc[place] + part[:, r * half : (r + 1) * half]
            if q == CHUNKS - 1:
                grads_ref[:, h * half : (h + 1) * half] = gacc[h]
    for copy in started:
        copy.wait_send()


def body(nx, ny, panels, chain_map, couplers, anc_band, anc_slot):
    ns, width = panels.shape[2], panels.shape[3]
    nr = couplers.shape[3]
    nz = lax.axis_size("sub")
    listed = anc_band.shape[1]
    half = width // 2
    sources = 2 * max(nx, ny)
    lanes = nr * half // 2
    mapmsg, symmsg = (width + PAD, width), (half + PAD, width)
    far = max(nx, ny)
    dma = lambda *shape: pltpu.SemaphoreType.DMA(shape)
    scratch = [
        pltpu.VMEM((ns * width, width), BF16),
        pltpu.VMEM((width, width), F32),
        pltpu.VMEM((nr * ns, width), BF16),
        pltpu.VMEM((listed, ns), jnp.int32),
        pltpu.VMEM((listed, ns), jnp.int32),
        pltpu.VMEM((width, width), F32),
        pltpu.VMEM((half, width), BF16),
        pltpu.VMEM((nz, 1, width), F32),
        pltpu.VMEM((nz, half // nz, width), BF16),
        pltpu.VMEM((half + 8, width), F32),
        pltpu.VMEM((half + 8, width), F32),
        pltpu.VMEM((width, width), F32),
        pltpu.VMEM((ny, *mapmsg), BF16),
        pltpu.VMEM((nx, *mapmsg), BF16),
        pltpu.VMEM((ny, *symmsg), BF16),
        pltpu.VMEM((nx, *symmsg), BF16),
        pltpu.VMEM((ny, width, 3 * width), BF16),
        pltpu.VMEM((ny, width, 3 * width), BF16),
        pltpu.VMEM((nx, width, 3 * width), BF16),
        pltpu.VMEM((width, width), F32),
        pltpu.VMEM((2, nr * ns, half), F32),
        pltpu.VMEM((nr * ns, width), F32),
        pltpu.VMEM((2, nr * ns, half), F32),
        pltpu.VMEM((2, nr * ns, 3 * width), BF16),
        pltpu.VMEM((3 * width, width), BF16),
        pltpu.VMEM((2 * nx, 8, sources * ns), jnp.int32),
        pltpu.VMEM((2 * ny, 8, sources * ns), jnp.int32),
        pltpu.VMEM((2, ns, lanes), BF16),
        pltpu.VMEM((2, ns, lanes), BF16),
        pltpu.VMEM((2 * nx * ns, lanes), BF16),
        pltpu.VMEM((2 * ny * ns, lanes), BF16),
        pltpu.VMEM((2 * ny * ns, 2 * ny * ns), BF16),
        pltpu.VMEM((2 * nx * ns, 2 * nx * ns), BF16),
        pltpu.VMEM((2 * ny * ns, lanes), BF16),
        pltpu.VMEM((2 * nx * ns, lanes), BF16),
        pltpu.VMEM((ny, 2, ns, lanes), BF16),
        pltpu.VMEM((nx, 2, ns, lanes), BF16),
        dma(8), dma(4),
        dma(nz), dma(nz), dma(nz), dma(nz), dma(nz), dma(nz),
        dma(2), dma(2),
        dma(2, ny), dma(2, ny), dma(2, nx), dma(2, nx),
        dma(2, far, 2), dma(2, far, 2),
        dma(CHUNKS, 2, far, 2), dma(CHUNKS, 2, far, 2), dma(CHUNKS, 2, far, 2), dma(CHUNKS, 2, far, 2),
    ]
    vmem = pl.BlockSpec(memory_space=pltpu.VMEM)
    hbm = pl.BlockSpec(memory_space=pl.ANY)
    front, grads = pl.pallas_call(
        functools.partial(kernel, nx, ny, nz, ns, nr),
        out_shape=(
            jax.ShapeDtypeStruct((width, width), F32),
            jax.ShapeDtypeStruct((ns * nr, width), F32),
        ),
        in_specs=[hbm] * 5,
        out_specs=(vmem, vmem),
        scratch_shapes=scratch,
        compiler_params=pltpu.CompilerParams(
            collective_id=0, has_side_effects=True, vmem_limit_bytes=48 * 2**20
        ),
        name="chain",
    )(
        *(
            pltpu.with_memory_space_constraint(array, pltpu.HBM)
            for array in (
                panels.reshape(ns * width, width),
                chain_map[0],
                couplers.reshape(ns * nr, width),
                anc_band.T,
                anc_slot.T,
            )
        )
    )
    return front[None], grads.reshape(1, 1, ns, nr, width)


def solution(mesh, nx=CHIPS_X, ny=CHIPS_Y):
    in_specs = (
        P("band", "sub", None, None, None),
        P("band", None, None),
        P("band", "sub", None, None, None),
        P(("band", "sub"), None),
        P(("band", "sub"), None),
    )
    out_specs = (P("band", None, None), P("band", "sub", None, None, None))
    return jax.shard_map(
        functools.partial(body, nx, ny), mesh=mesh, in_specs=in_specs, out_specs=out_specs, check_vma=False
    )
```

```python
import functools

import jax
import jax.numpy as jnp
from jax import lax
from jax.experimental import pallas as pl
from jax.experimental.pallas import tpu as pltpu
from jax.sharding import PartitionSpec as P

MESH = pl.DeviceIdType.MESH
F32, BF16 = jnp.float32, jnp.bfloat16
CHIPS_X, CHIPS_Y = 4, 4
PAD = 16
CHUNKS = 2
AHEAD = 3


def split(value):
    high = value.astype(BF16)
    return high, (value - high.astype(F32)).astype(BF16)


def dot(a, b):
    return jnp.dot(a, b, preferred_element_type=F32)


def dot_t(a, b):
    return lax.dot_general(a, b, (((1,), (1,)), ((), ())), preferred_element_type=F32)


def product(a, b):
    ah, al = split(a)
    bh, bl = split(b)
    return dot(ah, bh) + (dot(ah, bl) + dot(al, bh))


def product_t(a, b):
    ah, al = split(a)
    bh, bl = split(b)
    return dot_t(ah, bh) + (dot_t(ah, bl) + dot_t(al, bh))


def grid(shape, axis):
    return lax.broadcasted_iota(jnp.int32, shape, axis)


def diagonal(width):
    return grid((width, width), 0) == grid((width, width), 1)


def pick(block):
    return jnp.sum(jnp.where(diagonal(block.shape[0]), block, 0.0), axis=0, keepdims=True)


def pack_map(value, message):
    width = value.shape[1]
    high = value.astype(BF16)
    rest = pick(value - high.astype(F32))
    message[0:width, :] = high
    message[width : width + PAD, :] = jnp.broadcast_to(rest, (PAD, width)).astype(BF16)


def unpack_map(message):
    width = message.shape[1]
    rest = message[width : width + PAD, :].astype(F32)[0:1, :]
    return message[0:width, :].astype(F32) + jnp.where(diagonal(width), rest, 0.0)


def halves(full):
    half = full.shape[0] // 2
    upper = grid((half, half), 0) <= grid((half, half), 1)
    low = full[half:, half:]
    return full[:half, half:], jnp.where(upper, full[:half, :half], low), pick(low)


def halves_of_sum(full):
    half = full.shape[0] // 2
    rows, cols = grid((half, half), 0), grid((half, half), 1)
    first, low = full[:half, :half], full[half:, half:]
    side = full[:half, half:] + full[half:, :half].T
    mixed = jnp.where(rows <= cols, first, low) + jnp.where(rows >= cols, first, low).T
    return side, mixed, 2.0 * pick(low)


def one_sided(side, mixed, last):
    half = side.shape[0]
    rows, cols = grid((half, half), 0), grid((half, half), 1)
    middle = rows == cols
    first = jnp.where(rows < cols, mixed, jnp.where(middle, 0.5 * mixed, 0.0))
    low = jnp.where(rows > cols, mixed, jnp.where(middle, 0.5 * last, 0.0))
    top = jnp.concatenate([first, side], axis=1)
    return jnp.concatenate([top, jnp.concatenate([jnp.zeros_like(side), low], axis=1)], axis=0)


def parts_of(rows):
    half = rows.shape[1] // 2
    mixed = jnp.where(diagonal(half), rows[half : half + 1, 0:half], rows[0:half, half:])
    return rows[0:half, 0:half], mixed, rows[half : half + 1, half:]


def pack(parts, message):
    side, mixed, last = parts
    half = side.shape[0]
    message[0:half, 0:half] = side.astype(BF16)
    high = mixed.astype(BF16)
    message[0:half, half:] = high
    rest = pick(mixed - high.astype(F32))
    last_high = last.astype(BF16).astype(F32)
    row = grid((PAD, half), 0)
    message[half : half + PAD, 0:half] = jnp.where(row == 0, rest, 0.0).astype(BF16)
    tail = jnp.where(row == 0, last - last_high, jnp.where(row == 1, last_high, 0.0))
    message[half : half + PAD, half:] = tail.astype(BF16)


def unpack(message):
    half = message.shape[1] // 2
    tail = message[half : half + PAD, :].astype(F32)
    rest = tail[0:1, 0:half]
    mixed = message[0:half, half:].astype(F32) + jnp.where(diagonal(half), rest, 0.0)
    return message[0:half, 0:half].astype(F32), mixed, tail[0:1, half:] + tail[1:2, half:]


def far_first(count):
    return sorted(range(1, count), key=lambda d: -min(d, count - d))


def kernel(
    nx, ny, nz, ns, nr,
    panels, map_hbm, coup_hbm, band_hbm, slot_hbm,
    front_ref, grads_ref,
    pv, map_ref, coup_ref, band_ref, slot_ref, gram, shares, ends, rsbuf, upd, upd_other, map_other, abuf, bbuf, vbuf, tbuf,
    tcat, kcat, wcat, own_front, crm, cjm, gacc, ccat, fcat,
    keys0, keys1, xs0, xs1, x0, x1, sel0, sel1, o0, o1, rb0, rb1,
    psem, isem, rs_s, rs_r, dg_s, dg_r, ag_s, ag_r, c_s, c_r, y_s, y_r, x_s, x_r, k_s, k_r,
    s1_s, s1_r, s2_s, s2_r,
):
    width = map_ref.shape[0]
    half = width // 2
    slab = half // nz
    band, z = lax.axis_index("band"), lax.axis_index("sub")
    x, y, c = band // (2 * ny), (band // 2) % ny, band % 2

    def at(xx, yy, cc):
        return {"band": (xx * ny + yy) * 2 + cc}

    cores = (c, 1 - c)
    sibling = at(x, y, 1 - c)
    xpeer = {(d, e): at((x + d) % nx, y, cores[e]) for d in far_first(nx) for e in range(2)}
    ypeer = {(d, e): at(x, (y + d) % ny, cores[e]) for d in far_first(ny) for e in range(2)}
    zpeer = {d: {"sub": (z + d) % nz} for d in far_first(nz)}
    peers = [*zpeer.values(), *xpeer.values(), *ypeer.values(), sibling]
    started = []

    def send(src, dst, s, r, target):
        copy = pltpu.make_async_remote_copy(
            src_ref=src, dst_ref=dst, send_sem=s, recv_sem=r, device_id=target, device_id_type=MESH
        )
        copy.start()
        started.append(copy)
        return copy

    barrier = pltpu.get_barrier_semaphore()
    for peer in peers:
        pl.semaphore_signal(barrier, inc=1, device_id=peer, device_id_type=MESH)
    chunks = psem.shape[0]
    per = ns // chunks
    loads = []
    for q in range(chunks):
        rows = pl.ds(q * per * width, per * width)
        loads.append(pltpu.make_async_copy(panels.at[rows], pv.at[rows], psem.at[q]))
        if q < AHEAD:
            loads[-1].start()
        if q == 0:
            inputs = []
            small = ((coup_hbm, coup_ref), (map_hbm, map_ref), (band_hbm, band_ref), (slot_hbm, slot_ref))
            for n, (src, dst) in enumerate(small):
                inputs.append(pltpu.make_async_copy(src, dst, isem.at[n]))
                inputs[-1].start()
    inputs[0].wait()
    for q in range(chunks):
        loads[q].wait()
        if q + AHEAD < chunks:
            loads[q + AHEAD].start()
        block = pv[q * per * width : (q + 1) * per * width, :]
        part = dot(block.T, block)
        gram[...] = part if q == 0 else gram[...] + part
        for j in range(q * per, (q + 1) * per):
            value = dot(coup_ref[j * nr : (j + 1) * nr, :], pv[j * width : (j + 1) * width, :])
            cjm[j * nr : (j + 1) * nr, :] = value
            for h in range(2):
                crm[h, pl.ds(j, nr, stride=ns), :] = value[:, h * half : (h + 1) * half]
    side, mixed, last = halves(gram[...] * (1.0 / (nz * ns)))
    packed = jnp.concatenate([side, mixed], axis=1)
    gram[0:half, :] = packed
    shares[...] = packed.astype(BF16)
    ends[pl.ds(z, 1)] = jnp.concatenate([pick(mixed), last], axis=1)[None]
    for copy in inputs[1:]:
        copy.wait()
    pl.semaphore_wait(barrier, len(peers))

    rcopies = {
        d: send(shares.at[pl.ds(((z + d) % nz) * slab, slab)], rsbuf.at[d], rs_s.at[d], rs_r.at[d], peer)
        for d, peer in zpeer.items()
    }
    maps = send(map_ref, map_other, c_s.at[0], c_r.at[0], sibling)
    dcopies = [send(ends.at[z], ends.at[z], dg_s.at[d], dg_r.at[d], peer) for d, peer in zpeer.items()]
    p0, p1 = c * nx + x, c * ny + y
    keys = band_ref[...] * ns + slot_ref[...]
    keys = jnp.concatenate([keys, jnp.full((8 - keys.shape[0], ns), -1, jnp.int32)], axis=0)
    keys = jnp.concatenate([keys] * (keys0.shape[2] // ns), axis=1)
    keys0[pl.ds(p0, 1)] = keys[None]
    keys1[pl.ds(p1, 1)] = keys[None]
    own = keys0.at[p0]
    kcopies = [send(own, own, k_s.at[0, 0, 1], k_r.at[0, 0, 1], sibling)]
    for (d, e), peer in xpeer.items():
        kcopies.append(send(own, own, k_s.at[0, d, e], k_r.at[0, d, e], peer))
    own = keys1.at[p1]
    kcopies.append(send(own, own, k_s.at[1, 0, 1], k_r.at[1, 0, 1], sibling))
    for (d, e), peer in ypeer.items():
        kcopies.append(send(own, own, k_s.at[1, d, e], k_r.at[1, d, e], peer))
    maps.wait_recv()
    mine, other = map_ref[...], map_other[...]
    odd = jnp.where(c == 1, mine, other)
    even = jnp.where(c == 1, other, mine)
    identity = diagonal(width).astype(F32)
    pack_map(product(odd, even), abuf.at[y])
    acopies = [send(abuf.at[y], abuf.at[y], y_s.at[0, d], y_r.at[0, d], ypeer[d, 0]) for d in far_first(ny)]
    ch, cl = split(jnp.concatenate([crm[0], crm[1]], axis=1))
    ccat[0, :, 0:width], ccat[0, :, width : 2 * width], ccat[0, :, 2 * width :] = ch, ch, cl
    ch, cl = split(cjm[...])
    ccat[1, :, 0:width], ccat[1, :, width : 2 * width], ccat[1, :, 2 * width :] = ch, ch, cl
    own = pl.ds(pl.multiple_of(z * slab, slab), slab)
    total = gram[own, :]
    for d in range(1, nz):
        rcopies[d].wait_recv()
        total = total + rsbuf[d].astype(F32)
    upd[own, :] = total
    gcopies = [send(upd.at[own], upd.at[own], ag_s.at[d], ag_r.at[d], peer) for d, peer in zpeer.items()]
    for copy in dcopies:
        copy.wait_recv()
    last = ends[0]
    for m in range(1, nz):
        last = last + ends[m]
    upd[half : half + 8, :] = jnp.broadcast_to(last, (8, width))

    def fill(cat, index, value):
        high, low = split(value)
        cat[index, :, 0:width] = high
        cat[index, :, width : 2 * width] = high
        cat[index, :, 2 * width :] = low

    def term(cat, buffer, m, there=None):
        matrix = one_sided(*unpack(buffer.at[m]))
        high, low = split(matrix if there is None else jnp.where(there, matrix, 0.0))
        spread = cat[m]
        high, low = split(dot(spread, jnp.concatenate([high, low, high], axis=0)))
        return dot_t(jnp.concatenate([high, low, high], axis=1), spread)

    for copy in gcopies:
        copy.wait_recv()
    ucopy = send(upd, upd_other, c_s.at[1], c_r.at[1], sibling)
    ucopy.wait_recv()
    mine, other = upd[...], upd_other[...]
    upd_odd = jnp.where(c == 1, mine, other)
    upd_even = jnp.where(c == 1, other, mine)
    upd_even = one_sided(*parts_of(upd_even))
    side, mixed, last = halves_of_sum(product_t(product(odd, upd_even), odd))
    more = parts_of(upd_odd)
    pack((side + more[0], mixed + more[1], last + more[2]), vbuf.at[y])
    vcopies = {
        d: send(vbuf.at[y], vbuf.at[y], y_s.at[1, d], y_r.at[1, d], ypeer[d, 0]) for d in far_first(ny)
    }
    for copy in acopies:
        copy.wait_recv()
    group = [unpack_map(abuf.at[m]) for m in range(ny)]
    fill(tcat, ny - 1, identity)
    running = group[ny - 1]
    for m in range(ny - 2, -1, -1):
        fill(tcat, m, running)
        running = product(running, group[m])
    pack_map(running, bbuf.at[x])
    bcopies = {
        d: pltpu.make_async_remote_copy(
            src_ref=bbuf.at[x], dst_ref=bbuf.at[x], send_sem=x_s.at[0, d], recv_sem=x_r.at[0, d],
            device_id=xpeer[d, 0], device_id_type=MESH,
        )
        for d in far_first(nx)
    }
    for d, copy in bcopies.items():
        pl.when((x >= 1) & (x + d < nx))(copy.start)
    running = jnp.where(c == 1, even, identity)
    for m in range(ny - 2, -1, -1):
        fill(kcat, m, jnp.where(m < y, running, 0.0))
        running = product(running, jnp.where(m < y, group[m], identity))
    to_band = running
    fill(kcat, ny - 1, jnp.zeros_like(running))

    total = term(tcat, vbuf, y)
    for d in reversed(far_first(ny)):
        vcopies[d].wait_recv()
        total = total + term(tcat, vbuf, (y + ny - d) % ny)
    pack(halves_of_sum(total), tbuf.at[x])
    tcopies = {
        d: pltpu.make_async_remote_copy(
            src_ref=tbuf.at[x], dst_ref=tbuf.at[x], send_sem=x_s.at[1, d], recv_sem=x_r.at[1, d],
            device_id=xpeer[d, 0], device_id_type=MESH,
        )
        for d in far_first(nx)
    }
    for d, copy in tcopies.items():
        pl.when(x + d < nx)(copy.start)
    total = jnp.where(c == 1, upd_even, 0.0)
    for d in range(1, ny):
        total = total + term(kcat, vbuf, (y + ny - d) % ny)
    own_front[...] = total
    for d, copy in bcopies.items():
        pl.when(x >= d + 1)(copy.wait_recv)
    running = to_band
    fill(wcat, nx - 1, jnp.zeros_like(running))
    for m in range(nx - 2, -1, -1):
        fill(wcat, m, jnp.where(m < x, running, 0.0))
        if m:
            running = product(running, jnp.where(m < x, unpack_map(bbuf.at[m]), identity))
    for copy in kcopies:
        copy.wait_recv()

    def selection(keys, count, band_of):
        rows, lanes = 2 * count * ns, 2 * count * ns
        lane = grid((8, lanes), 1) // ns
        merged = jnp.zeros((8, lanes), jnp.int32)
        for p in range(2 * count):
            merged = jnp.where(lane == p, keys[p, :, 0:lanes], merged)
        row = grid((rows, lanes), 0)
        wanted = row % ns
        for p in range(2 * count):
            target = band_of(p % count, p // count)["band"]
            wanted = wanted + jnp.where(row // ns == p, target * ns, 0)
        hits = jnp.zeros((rows, lanes), F32)
        for k in range(4):
            hits = hits + jnp.where(merged[k : k + 1, :] == wanted, 1.0, 0.0)
        return hits.astype(BF16)

    sel0[...] = selection(keys0, ny, lambda m, core: at(x, m, core))
    sel1[...] = selection(keys1, nx, lambda m, core: at(m, y, core))
    front = own_front[...]
    for d, copy in tcopies.items():
        pl.when(x >= d)(copy.wait_recv)
    for d in range(1, nx):
        front = front + term(wcat, tbuf, (x + nx - d) % nx, x >= d)
    front = front + front.T
    front_ref[...] = front

    fh, fl = split(front)
    fcat[0:width, :], fcat[width : 2 * width, :], fcat[2 * width :, :] = fh, fl, fh
    lanes = nr * half // 2
    piece = lanes // CHUNKS
    own0 = pl.ds(pl.multiple_of(p0 * ns, ns), ns)
    own1 = pl.ds(pl.multiple_of(p1 * ns, ns), ns)
    gathers = []
    for q in range(CHUNKS):
        span = pl.ds(q * piece, piece)
        for core in range(2):
            first = (core * CHUNKS + q) * (nr // 2 // CHUNKS)
            count = nr // 2 // CHUNKS
            sent = dot(ccat[0, first * ns : (first + count) * ns, :], fcat[...]).astype(BF16)
            for r in range(count):
                place = slice(q * piece + r * half, q * piece + (r + 1) * half)
                xs0[core, :, place] = sent[r * ns : (r + 1) * ns, 0:half]
                xs1[core, :, place] = sent[r * ns : (r + 1) * ns, half:]
        batch = {}
        for h, xs, xx, rows, all_peers in ((0, xs0, x0, own0, xpeer), (1, xs1, x1, own1, ypeer)):
            batch[h] = []
            targets = {**all_peers, (0, 1): sibling}
            for (d, e), peer in targets.items():
                batch[h].append(
                    send(
                        xs.at[cores[e], :, span], xx.at[rows, span],
                        s1_s.at[q, h, d, e], s1_r.at[q, h, d, e], peer,
                    )
                )
            xx[rows, span] = xs[c, :, span]
        gathers.append(batch)
    adjoint = dot(ccat[1], fcat[...])
    for h in range(2):
        gacc[h] = adjoint[:, h * half : (h + 1) * half]
    scatters = {}
    for q in range(CHUNKS):
        for h, sel, xx, oo, rb, count, all_peers in (
            (0, sel0, x0, o0, rb0, ny, ypeer), (1, sel1, x1, o1, rb1, nx, xpeer),
        ):
            here = (y, x)[h]
            for copy in gathers[q][h]:
                copy.wait_recv()
            for first in range(q * piece, (q + 1) * piece, width):
                span = slice(first, first + width)
                oo[:, span] = dot(sel[...], xx[:, span]).astype(BF16)
            span = pl.ds(q * piece, piece)
            scatters[q, h] = []
            for (d, e), peer in {**all_peers, (0, 1): sibling}.items():
                rows = pl.ds(pl.multiple_of((cores[e] * count + (here + d) % count) * ns, ns), ns)
                scatters[q, h].append(
                    send(
                        oo.at[rows, span], rb.at[d, e, :, span],
                        s2_s.at[q, h, d, e], s2_r.at[q, h, d, e], peer,
                    )
                )
    for q in range(CHUNKS):
        for h, oo, rb, count, here in ((0, o0, rb0, ny, y), (1, o1, rb1, nx, x)):
            for copy in scatters[q, h]:
                copy.wait_recv()
            span = pl.ds(q * piece, piece)
            rows = pl.ds(pl.multiple_of((c * count + here) * ns, ns), ns)
            same, cross = oo[rows, span].astype(F32), rb[0, 1, :, span].astype(F32)
            for d in range(1, count):
                same, cross = same + rb[d, 0, :, span].astype(F32), cross + rb[d, 1, :, span].astype(F32)
            for core, part in enumerate((jnp.where(c == 0, same, cross), jnp.where(c == 0, cross, same))):
                for r in range(piece // half):
                    place = (h, pl.ds((core * CHUNKS + q) * (piece // half) + r, ns, stride=nr), slice(None))
                    gacc[place] = gacc[place] + part[:, r * half : (r + 1) * half]
            if q == CHUNKS - 1:
                grads_ref[:, h * half : (h + 1) * half] = gacc[h]
    for copy in started:
        copy.wait_send()
    for d in far_first(nx):
        pl.when(x + d < nx)(tcopies[d].wait_send)
        pl.when((x >= 1) & (x + d < nx))(bcopies[d].wait_send)


def body(nx, ny, panels, chain_map, couplers, anc_band, anc_slot):
    ns, width = panels.shape[2], panels.shape[3]
    nr = couplers.shape[3]
    nz = lax.axis_size("sub")
    listed = anc_band.shape[1]
    half = width // 2
    sources = 2 * max(nx, ny)
    lanes = nr * half // 2
    mapmsg, symmsg = (width + PAD, width), (half + PAD, width)
    far = max(nx, ny)
    dma = lambda *shape: pltpu.SemaphoreType.DMA(shape)
    scratch = [
        pltpu.VMEM((ns * width, width), BF16),
        pltpu.VMEM((width, width), F32),
        pltpu.VMEM((nr * ns, width), BF16),
        pltpu.VMEM((listed, ns), jnp.int32),
        pltpu.VMEM((listed, ns), jnp.int32),
        pltpu.VMEM((width, width), F32),
        pltpu.VMEM((half, width), BF16),
        pltpu.VMEM((nz, 1, width), F32),
        pltpu.VMEM((nz, half // nz, width), BF16),
        pltpu.VMEM((half + 8, width), F32),
        pltpu.VMEM((half + 8, width), F32),
        pltpu.VMEM((width, width), F32),
        pltpu.VMEM((ny, *mapmsg), BF16),
        pltpu.VMEM((nx, *mapmsg), BF16),
        pltpu.VMEM((ny, *symmsg), BF16),
        pltpu.VMEM((nx, *symmsg), BF16),
        pltpu.VMEM((ny, width, 3 * width), BF16),
        pltpu.VMEM((ny, width, 3 * width), BF16),
        pltpu.VMEM((nx, width, 3 * width), BF16),
        pltpu.VMEM((width, width), F32),
        pltpu.VMEM((2, nr * ns, half), F32),
        pltpu.VMEM((nr * ns, width), F32),
        pltpu.VMEM((2, nr * ns, half), F32),
        pltpu.VMEM((2, nr * ns, 3 * width), BF16),
        pltpu.VMEM((3 * width, width), BF16),
        pltpu.VMEM((2 * nx, 8, sources * ns), jnp.int32),
        pltpu.VMEM((2 * ny, 8, sources * ns), jnp.int32),
        pltpu.VMEM((2, ns, lanes), BF16),
        pltpu.VMEM((2, ns, lanes), BF16),
        pltpu.VMEM((2 * nx * ns, lanes), BF16),
        pltpu.VMEM((2 * ny * ns, lanes), BF16),
        pltpu.VMEM((2 * ny * ns, 2 * ny * ns), BF16),
        pltpu.VMEM((2 * nx * ns, 2 * nx * ns), BF16),
        pltpu.VMEM((2 * ny * ns, lanes), BF16),
        pltpu.VMEM((2 * nx * ns, lanes), BF16),
        pltpu.VMEM((ny, 2, ns, lanes), BF16),
        pltpu.VMEM((nx, 2, ns, lanes), BF16),
        dma(8), dma(4),
        dma(nz), dma(nz), dma(nz), dma(nz), dma(nz), dma(nz),
        dma(2), dma(2),
        dma(2, ny), dma(2, ny), dma(2, nx), dma(2, nx),
        dma(2, far, 2), dma(2, far, 2),
        dma(CHUNKS, 2, far, 2), dma(CHUNKS, 2, far, 2), dma(CHUNKS, 2, far, 2), dma(CHUNKS, 2, far, 2),
    ]
    vmem = pl.BlockSpec(memory_space=pltpu.VMEM)
    hbm = pl.BlockSpec(memory_space=pl.ANY)
    front, grads = pl.pallas_call(
        functools.partial(kernel, nx, ny, nz, ns, nr),
        out_shape=(
            jax.ShapeDtypeStruct((width, width), F32),
            jax.ShapeDtypeStruct((ns * nr, width), F32),
        ),
        in_specs=[hbm] * 5,
        out_specs=(vmem, vmem),
        scratch_shapes=scratch,
        compiler_params=pltpu.CompilerParams(
            collective_id=0, has_side_effects=True, vmem_limit_bytes=48 * 2**20
        ),
        name="chain",
    )(
        *(
            pltpu.with_memory_space_constraint(array, pltpu.HBM)
            for array in (
                panels.reshape(ns * width, width),
                chain_map[0],
                couplers.reshape(ns * nr, width),
                anc_band.T,
                anc_slot.T,
            )
        )
    )
    return front[None], grads.reshape(1, 1, ns, nr, width)


def solution(mesh, nx=CHIPS_X, ny=CHIPS_Y):
    in_specs = (
        P("band", "sub", None, None, None),
        P("band", None, None),
        P("band", "sub", None, None, None),
        P(("band", "sub"), None),
        P(("band", "sub"), None),
    )
    out_specs = (P("band", None, None), P("band", "sub", None, None, None))
    return jax.shard_map(
        functools.partial(body, nx, ny), mesh=mesh, in_specs=in_specs, out_specs=out_specs, check_vma=False
    )
```

```python
import functools

import jax
import jax.numpy as jnp
from jax import lax
from jax.experimental import pallas as pl
from jax.experimental.pallas import tpu as pltpu
from jax.sharding import PartitionSpec as P

MESH = pl.DeviceIdType.MESH
F32, BF16 = jnp.float32, jnp.bfloat16
CHIPS_X, CHIPS_Y = 4, 4
PAD = 16
CHUNKS = 2
AHEAD = 3


def split(value):
    high = value.astype(BF16)
    return high, (value - high.astype(F32)).astype(BF16)


def dot(a, b):
    return jnp.dot(a, b, preferred_element_type=F32)


def dot_t(a, b):
    return lax.dot_general(a, b, (((1,), (1,)), ((), ())), preferred_element_type=F32)


def product(a, b):
    ah, al = split(a)
    bh, bl = split(b)
    return dot(ah, bh) + (dot(ah, bl) + dot(al, bh))


def product_t(a, b):
    ah, al = split(a)
    bh, bl = split(b)
    return dot_t(ah, bh) + (dot_t(ah, bl) + dot_t(al, bh))


def grid(shape, axis):
    return lax.broadcasted_iota(jnp.int32, shape, axis)


def diagonal(width):
    return grid((width, width), 0) == grid((width, width), 1)


def pick(block):
    return jnp.sum(jnp.where(diagonal(block.shape[0]), block, 0.0), axis=0, keepdims=True)


def pack_map(value, message):
    width = value.shape[1]
    high = value.astype(BF16)
    rest = pick(value - high.astype(F32))
    message[0:width, :] = high
    message[width : width + PAD, :] = jnp.broadcast_to(rest, (PAD, width)).astype(BF16)


def unpack_map(message):
    width = message.shape[1]
    rest = message[width : width + PAD, :].astype(F32)[0:1, :]
    return message[0:width, :].astype(F32) + jnp.where(diagonal(width), rest, 0.0)


def halves(full):
    half = full.shape[0] // 2
    upper = grid((half, half), 0) <= grid((half, half), 1)
    low = full[half:, half:]
    return full[:half, half:], jnp.where(upper, full[:half, :half], low), pick(low)


def halves_of_sum(full):
    half = full.shape[0] // 2
    rows, cols = grid((half, half), 0), grid((half, half), 1)
    first, low = full[:half, :half], full[half:, half:]
    side = full[:half, half:] + full[half:, :half].T
    mixed = jnp.where(rows <= cols, first, low) + jnp.where(rows >= cols, first, low).T
    return side, mixed, 2.0 * pick(low)


def one_sided(side, mixed, last):
    half = side.shape[0]
    rows, cols = grid((half, half), 0), grid((half, half), 1)
    middle = rows == cols
    first = jnp.where(rows < cols, mixed, jnp.where(middle, 0.5 * mixed, 0.0))
    low = jnp.where(rows > cols, mixed, jnp.where(middle, 0.5 * last, 0.0))
    top = jnp.concatenate([first, side], axis=1)
    return jnp.concatenate([top, jnp.concatenate([jnp.zeros_like(side), low], axis=1)], axis=0)


def parts_of(rows):
    half = rows.shape[1] // 2
    mixed = jnp.where(diagonal(half), rows[half : half + 1, 0:half], rows[0:half, half:])
    return rows[0:half, 0:half], mixed, rows[half : half + 1, half:]


def pack(parts, message):
    side, mixed, last = parts
    half = side.shape[0]
    message[0:half, 0:half] = side.astype(BF16)
    high = mixed.astype(BF16)
    message[0:half, half:] = high
    rest = pick(mixed - high.astype(F32))
    last_high = last.astype(BF16).astype(F32)
    row = grid((PAD, half), 0)
    message[half : half + PAD, 0:half] = jnp.where(row == 0, rest, 0.0).astype(BF16)
    tail = jnp.where(row == 0, last - last_high, jnp.where(row == 1, last_high, 0.0))
    message[half : half + PAD, half:] = tail.astype(BF16)


def unpack(message):
    half = message.shape[1] // 2
    tail = message[half : half + PAD, :].astype(F32)
    rest = tail[0:1, 0:half]
    mixed = message[0:half, half:].astype(F32) + jnp.where(diagonal(half), rest, 0.0)
    return message[0:half, 0:half].astype(F32), mixed, tail[0:1, half:] + tail[1:2, half:]


def far_first(count):
    return sorted(range(1, count), key=lambda d: -min(d, count - d))


def kernel(
    nx, ny, nz, ns, nr,
    panels, map_hbm, coup_hbm, band_hbm, slot_hbm,
    front_ref, grads_ref,
    pv, map_ref, coup_ref, band_ref, slot_ref, gram, shares, ends, rsbuf, upd, upd_other, map_other, abuf, bbuf, vbuf, tbuf,
    tcat, kcat, wcat, own_front, crm, cjm, gacc, ccat, fcat,
    keys0, keys1, xs0, xs1, x0, x1, sel0, sel1, o0, o1, rb0, rb1,
    psem, isem, rs_s, rs_r, dg_s, dg_r, ag_s, ag_r, c_s, c_r, y_s, y_r, x_s, x_r, k_s, k_r,
    s1_s, s1_r, s2_s, s2_r,
):
    width = map_ref.shape[0]
    half = width // 2
    slab = half // nz
    band, z = lax.axis_index("band"), lax.axis_index("sub")
    x, y, c = band // (2 * ny), (band // 2) % ny, band % 2

    def at(xx, yy, cc):
        return {"band": (xx * ny + yy) * 2 + cc}

    cores = (c, 1 - c)
    sibling = at(x, y, 1 - c)
    xpeer = {(d, e): at((x + d) % nx, y, cores[e]) for d in far_first(nx) for e in range(2)}
    ypeer = {(d, e): at(x, (y + d) % ny, cores[e]) for d in far_first(ny) for e in range(2)}
    zpeer = {d: {"sub": (z + d) % nz} for d in far_first(nz)}
    peers = [*zpeer.values(), *xpeer.values(), *ypeer.values(), sibling]
    started = []

    def send(src, dst, s, r, target):
        copy = pltpu.make_async_remote_copy(
            src_ref=src, dst_ref=dst, send_sem=s, recv_sem=r, device_id=target, device_id_type=MESH
        )
        copy.start()
        started.append(copy)
        return copy

    barrier = pltpu.get_barrier_semaphore()
    for peer in peers:
        pl.semaphore_signal(barrier, inc=1, device_id=peer, device_id_type=MESH)
    chunks = psem.shape[0]
    per = ns // chunks
    loads = []
    for q in range(chunks):
        rows = pl.ds(q * per * width, per * width)
        loads.append(pltpu.make_async_copy(panels.at[rows], pv.at[rows], psem.at[q]))
        if q < AHEAD:
            loads[-1].start()
        if q == 0:
            inputs = []
            small = ((coup_hbm, coup_ref), (map_hbm, map_ref), (band_hbm, band_ref), (slot_hbm, slot_ref))
            for n, (src, dst) in enumerate(small):
                inputs.append(pltpu.make_async_copy(src, dst, isem.at[n]))
                inputs[-1].start()
    inputs[0].wait()
    for q in range(chunks):
        loads[q].wait()
        if q + AHEAD < chunks:
            loads[q + AHEAD].start()
        block = pv[q * per * width : (q + 1) * per * width, :]
        part = dot(block.T, block)
        gram[...] = part if q == 0 else gram[...] + part
    side, mixed, last = halves(gram[...] * (1.0 / (nz * ns)))
    packed = jnp.concatenate([side, mixed], axis=1)
    gram[0:half, :] = packed
    shares[...] = packed.astype(BF16)
    ends[pl.ds(z, 1)] = jnp.concatenate([pick(mixed), last], axis=1)[None]
    for copy in inputs[1:]:
        copy.wait()
    pl.semaphore_wait(barrier, len(peers))

    rcopies = {
        d: send(shares.at[pl.ds(((z + d) % nz) * slab, slab)], rsbuf.at[d], rs_s.at[d], rs_r.at[d], peer)
        for d, peer in zpeer.items()
    }
    maps = send(map_ref, map_other, c_s.at[0], c_r.at[0], sibling)
    dcopies = [send(ends.at[z], ends.at[z], dg_s.at[d], dg_r.at[d], peer) for d, peer in zpeer.items()]
    p0, p1 = c * nx + x, c * ny + y
    keys = band_ref[...] * ns + slot_ref[...]
    keys = jnp.concatenate([keys, jnp.full((8 - keys.shape[0], ns), -1, jnp.int32)], axis=0)
    keys = jnp.concatenate([keys] * (keys0.shape[2] // ns), axis=1)
    keys0[pl.ds(p0, 1)] = keys[None]
    keys1[pl.ds(p1, 1)] = keys[None]
    own = keys0.at[p0]
    kcopies = [send(own, own, k_s.at[0, 0, 1], k_r.at[0, 0, 1], sibling)]
    for (d, e), peer in xpeer.items():
        kcopies.append(send(own, own, k_s.at[0, d, e], k_r.at[0, d, e], peer))
    own = keys1.at[p1]
    kcopies.append(send(own, own, k_s.at[1, 0, 1], k_r.at[1, 0, 1], sibling))
    for (d, e), peer in ypeer.items():
        kcopies.append(send(own, own, k_s.at[1, d, e], k_r.at[1, d, e], peer))
    for j in range(ns):
        value = dot(coup_ref[j * nr : (j + 1) * nr, :], pv[j * width : (j + 1) * width, :])
        cjm[j * nr : (j + 1) * nr, :] = value
        for h in range(2):
            crm[h, pl.ds(j, nr, stride=ns), :] = value[:, h * half : (h + 1) * half]
    maps.wait_recv()
    mine, other = map_ref[...], map_other[...]
    odd = jnp.where(c == 1, mine, other)
    even = jnp.where(c == 1, other, mine)
    identity = diagonal(width).astype(F32)
    pack_map(product(odd, even), abuf.at[y])
    acopies = [send(abuf.at[y], abuf.at[y], y_s.at[0, d], y_r.at[0, d], ypeer[d, 0]) for d in far_first(ny)]
    ch, cl = split(jnp.concatenate([crm[0], crm[1]], axis=1))
    ccat[0, :, 0:width], ccat[0, :, width : 2 * width], ccat[0, :, 2 * width :] = ch, ch, cl
    ch, cl = split(cjm[...])
    ccat[1, :, 0:width], ccat[1, :, width : 2 * width], ccat[1, :, 2 * width :] = ch, ch, cl
    own = pl.ds(pl.multiple_of(z * slab, slab), slab)
    total = gram[own, :]
    for d in range(1, nz):
        rcopies[d].wait_recv()
        total = total + rsbuf[d].astype(F32)
    upd[own, :] = total
    gcopies = [send(upd.at[own], upd.at[own], ag_s.at[d], ag_r.at[d], peer) for d, peer in zpeer.items()]
    for copy in dcopies:
        copy.wait_recv()
    last = ends[0]
    for m in range(1, nz):
        last = last + ends[m]
    upd[half : half + 8, :] = jnp.broadcast_to(last, (8, width))

    def fill(cat, index, value):
        high, low = split(value)
        cat[index, :, 0:width] = high
        cat[index, :, width : 2 * width] = high
        cat[index, :, 2 * width :] = low

    def term(cat, buffer, m, there=None):
        matrix = one_sided(*unpack(buffer.at[m]))
        high, low = split(matrix if there is None else jnp.where(there, matrix, 0.0))
        spread = cat[m]
        high, low = split(dot(spread, jnp.concatenate([high, low, high], axis=0)))
        return dot_t(jnp.concatenate([high, low, high], axis=1), spread)

    for copy in gcopies:
        copy.wait_recv()
    ucopy = send(upd, upd_other, c_s.at[1], c_r.at[1], sibling)
    ucopy.wait_recv()
    mine, other = upd[...], upd_other[...]
    upd_odd = jnp.where(c == 1, mine, other)
    upd_even = jnp.where(c == 1, other, mine)
    upd_even = one_sided(*parts_of(upd_even))
    side, mixed, last = halves_of_sum(product_t(product(odd, upd_even), odd))
    more = parts_of(upd_odd)
    pack((side + more[0], mixed + more[1], last + more[2]), vbuf.at[y])
    vcopies = {
        d: send(vbuf.at[y], vbuf.at[y], y_s.at[1, d], y_r.at[1, d], ypeer[d, 0]) for d in far_first(ny)
    }
    for copy in acopies:
        copy.wait_recv()
    group = [unpack_map(abuf.at[m]) for m in range(ny)]
    fill(tcat, ny - 1, identity)
    running = group[ny - 1]
    for m in range(ny - 2, -1, -1):
        fill(tcat, m, running)
        running = product(running, group[m])
    pack_map(running, bbuf.at[x])
    bcopies = {
        d: pltpu.make_async_remote_copy(
            src_ref=bbuf.at[x], dst_ref=bbuf.at[x], send_sem=x_s.at[0, d], recv_sem=x_r.at[0, d],
            device_id=xpeer[d, 0], device_id_type=MESH,
        )
        for d in far_first(nx)
    }
    for d, copy in bcopies.items():
        pl.when((x >= 1) & (x + d < nx))(copy.start)
    running = jnp.where(c == 1, even, identity)
    for m in range(ny - 2, -1, -1):
        fill(kcat, m, jnp.where(m < y, running, 0.0))
        running = product(running, jnp.where(m < y, group[m], identity))
    to_band = running
    fill(kcat, ny - 1, jnp.zeros_like(running))

    total = term(tcat, vbuf, y)
    for copy in vcopies.values():
        copy.wait_recv()
    for d in range(1, ny):
        total = total + term(tcat, vbuf, (y + ny - d) % ny)
    pack(halves_of_sum(total), tbuf.at[x])
    tcopies = {
        d: pltpu.make_async_remote_copy(
            src_ref=tbuf.at[x], dst_ref=tbuf.at[x], send_sem=x_s.at[1, d], recv_sem=x_r.at[1, d],
            device_id=xpeer[d, 0], device_id_type=MESH,
        )
        for d in far_first(nx)
    }
    for d, copy in tcopies.items():
        pl.when(x + d < nx)(copy.start)
    total = jnp.where(c == 1, upd_even, 0.0)
    for d in range(1, ny):
        total = total + term(kcat, vbuf, (y + ny - d) % ny)
    own_front[...] = total
    for d, copy in bcopies.items():
        pl.when(x >= d + 1)(copy.wait_recv)
    running = to_band
    fill(wcat, nx - 1, jnp.zeros_like(running))
    for m in range(nx - 2, -1, -1):
        fill(wcat, m, jnp.where(m < x, running, 0.0))
        if m:
            running = product(running, jnp.where(m < x, unpack_map(bbuf.at[m]), identity))
    for copy in kcopies:
        copy.wait_recv()

    def selection(keys, count, band_of):
        rows, lanes = 2 * count * ns, 2 * count * ns
        lane = grid((8, lanes), 1) // ns
        merged = jnp.zeros((8, lanes), jnp.int32)
        for p in range(2 * count):
            merged = jnp.where(lane == p, keys[p, :, 0:lanes], merged)
        row = grid((rows, lanes), 0)
        wanted = row % ns
        for p in range(2 * count):
            target = band_of(p % count, p // count)["band"]
            wanted = wanted + jnp.where(row // ns == p, target * ns, 0)
        hits = jnp.zeros((rows, lanes), F32)
        for k in range(4):
            hits = hits + jnp.where(merged[k : k + 1, :] == wanted, 1.0, 0.0)
        return hits.astype(BF16)

    sel0[...] = selection(keys0, ny, lambda m, core: at(x, m, core))
    sel1[...] = selection(keys1, nx, lambda m, core: at(m, y, core))
    front = own_front[...]
    for d, copy in tcopies.items():
        pl.when(x >= d)(copy.wait_recv)
    for d in range(1, nx):
        front = front + term(wcat, tbuf, (x + nx - d) % nx, x >= d)
    front = front + front.T
    front_ref[...] = front

    fh, fl = split(front)
    fcat[0:width, :], fcat[width : 2 * width, :], fcat[2 * width :, :] = fh, fl, fh
    lanes = nr * half // 2
    piece = lanes // CHUNKS
    own0 = pl.ds(pl.multiple_of(p0 * ns, ns), ns)
    own1 = pl.ds(pl.multiple_of(p1 * ns, ns), ns)
    gathers = []
    for q in range(CHUNKS):
        span = pl.ds(q * piece, piece)
        for core in range(2):
            first = (core * CHUNKS + q) * (nr // 2 // CHUNKS)
            count = nr // 2 // CHUNKS
            sent = dot(ccat[0, first * ns : (first + count) * ns, :], fcat[...]).astype(BF16)
            for r in range(count):
                place = slice(q * piece + r * half, q * piece + (r + 1) * half)
                xs0[core, :, place] = sent[r * ns : (r + 1) * ns, 0:half]
                xs1[core, :, place] = sent[r * ns : (r + 1) * ns, half:]
        batch = {}
        for h, xs, xx, rows, all_peers in ((0, xs0, x0, own0, xpeer), (1, xs1, x1, own1, ypeer)):
            batch[h] = []
            targets = {**all_peers, (0, 1): sibling}
            for (d, e), peer in targets.items():
                batch[h].append(
                    send(
                        xs.at[cores[e], :, span], xx.at[rows, span],
                        s1_s.at[q, h, d, e], s1_r.at[q, h, d, e], peer,
                    )
                )
            xx[rows, span] = xs[c, :, span]
        gathers.append(batch)
    adjoint = dot(ccat[1], fcat[...])
    for h in range(2):
        gacc[h] = adjoint[:, h * half : (h + 1) * half]
    scatters = {}
    for q in range(CHUNKS):
        for h, sel, xx, oo, rb, count, all_peers in (
            (0, sel0, x0, o0, rb0, ny, ypeer), (1, sel1, x1, o1, rb1, nx, xpeer),
        ):
            here = (y, x)[h]
            for copy in gathers[q][h]:
                copy.wait_recv()
            for first in range(q * piece, (q + 1) * piece, width):
                span = slice(first, first + width)
                oo[:, span] = dot(sel[...], xx[:, span]).astype(BF16)
            span = pl.ds(q * piece, piece)
            scatters[q, h] = []
            for (d, e), peer in {**all_peers, (0, 1): sibling}.items():
                rows = pl.ds(pl.multiple_of((cores[e] * count + (here + d) % count) * ns, ns), ns)
                scatters[q, h].append(
                    send(
                        oo.at[rows, span], rb.at[d, e, :, span],
                        s2_s.at[q, h, d, e], s2_r.at[q, h, d, e], peer,
                    )
                )
    for q in range(CHUNKS):
        for h, oo, rb, count, here in ((0, o0, rb0, ny, y), (1, o1, rb1, nx, x)):
            for copy in scatters[q, h]:
                copy.wait_recv()
            span = pl.ds(q * piece, piece)
            rows = pl.ds(pl.multiple_of((c * count + here) * ns, ns), ns)
            same, cross = oo[rows, span].astype(F32), rb[0, 1, :, span].astype(F32)
            for d in range(1, count):
                same, cross = same + rb[d, 0, :, span].astype(F32), cross + rb[d, 1, :, span].astype(F32)
            for core, part in enumerate((jnp.where(c == 0, same, cross), jnp.where(c == 0, cross, same))):
                for r in range(piece // half):
                    place = (h, pl.ds((core * CHUNKS + q) * (piece // half) + r, ns, stride=nr), slice(None))
                    gacc[place] = gacc[place] + part[:, r * half : (r + 1) * half]
            if q == CHUNKS - 1:
                grads_ref[:, h * half : (h + 1) * half] = gacc[h]
    for copy in started:
        copy.wait_send()
    for d in far_first(nx):
        pl.when(x + d < nx)(tcopies[d].wait_send)
        pl.when((x >= 1) & (x + d < nx))(bcopies[d].wait_send)


def body(nx, ny, panels, chain_map, couplers, anc_band, anc_slot):
    ns, width = panels.shape[2], panels.shape[3]
    nr = couplers.shape[3]
    nz = lax.axis_size("sub")
    listed = anc_band.shape[1]
    half = width // 2
    sources = 2 * max(nx, ny)
    lanes = nr * half // 2
    mapmsg, symmsg = (width + PAD, width), (half + PAD, width)
    far = max(nx, ny)
    dma = lambda *shape: pltpu.SemaphoreType.DMA(shape)
    scratch = [
        pltpu.VMEM((ns * width, width), BF16),
        pltpu.VMEM((width, width), F32),
        pltpu.VMEM((nr * ns, width), BF16),
        pltpu.VMEM((listed, ns), jnp.int32),
        pltpu.VMEM((listed, ns), jnp.int32),
        pltpu.VMEM((width, width), F32),
        pltpu.VMEM((half, width), BF16),
        pltpu.VMEM((nz, 1, width), F32),
        pltpu.VMEM((nz, half // nz, width), BF16),
        pltpu.VMEM((half + 8, width), F32),
        pltpu.VMEM((half + 8, width), F32),
        pltpu.VMEM((width, width), F32),
        pltpu.VMEM((ny, *mapmsg), BF16),
        pltpu.VMEM((nx, *mapmsg), BF16),
        pltpu.VMEM((ny, *symmsg), BF16),
        pltpu.VMEM((nx, *symmsg), BF16),
        pltpu.VMEM((ny, width, 3 * width), BF16),
        pltpu.VMEM((ny, width, 3 * width), BF16),
        pltpu.VMEM((nx, width, 3 * width), BF16),
        pltpu.VMEM((width, width), F32),
        pltpu.VMEM((2, nr * ns, half), F32),
        pltpu.VMEM((nr * ns, width), F32),
        pltpu.VMEM((2, nr * ns, half), F32),
        pltpu.VMEM((2, nr * ns, 3 * width), BF16),
        pltpu.VMEM((3 * width, width), BF16),
        pltpu.VMEM((2 * nx, 8, sources * ns), jnp.int32),
        pltpu.VMEM((2 * ny, 8, sources * ns), jnp.int32),
        pltpu.VMEM((2, ns, lanes), BF16),
        pltpu.VMEM((2, ns, lanes), BF16),
        pltpu.VMEM((2 * nx * ns, lanes), BF16),
        pltpu.VMEM((2 * ny * ns, lanes), BF16),
        pltpu.VMEM((2 * ny * ns, 2 * ny * ns), BF16),
        pltpu.VMEM((2 * nx * ns, 2 * nx * ns), BF16),
        pltpu.VMEM((2 * ny * ns, lanes), BF16),
        pltpu.VMEM((2 * nx * ns, lanes), BF16),
        pltpu.VMEM((ny, 2, ns, lanes), BF16),
        pltpu.VMEM((nx, 2, ns, lanes), BF16),
        dma(8), dma(4),
        dma(nz), dma(nz), dma(nz), dma(nz), dma(nz), dma(nz),
        dma(2), dma(2),
        dma(2, ny), dma(2, ny), dma(2, nx), dma(2, nx),
        dma(2, far, 2), dma(2, far, 2),
        dma(CHUNKS, 2, far, 2), dma(CHUNKS, 2, far, 2), dma(CHUNKS, 2, far, 2), dma(CHUNKS, 2, far, 2),
    ]
    vmem = pl.BlockSpec(memory_space=pltpu.VMEM)
    hbm = pl.BlockSpec(memory_space=pl.ANY)
    front, grads = pl.pallas_call(
        functools.partial(kernel, nx, ny, nz, ns, nr),
        out_shape=(
            jax.ShapeDtypeStruct((width, width), F32),
            jax.ShapeDtypeStruct((ns * nr, width), F32),
        ),
        in_specs=[hbm] * 5,
        out_specs=(vmem, vmem),
        scratch_shapes=scratch,
        compiler_params=pltpu.CompilerParams(
            collective_id=0, has_side_effects=True, vmem_limit_bytes=48 * 2**20
        ),
        name="chain",
    )(
        *(
            pltpu.with_memory_space_constraint(array, pltpu.HBM)
            for array in (
                panels.reshape(ns * width, width),
                chain_map[0],
                couplers.reshape(ns * nr, width),
                anc_band.T,
                anc_slot.T,
            )
        )
    )
    return front[None], grads.reshape(1, 1, ns, nr, width)


def solution(mesh, nx=CHIPS_X, ny=CHIPS_Y):
    in_specs = (
        P("band", "sub", None, None, None),
        P("band", None, None),
        P("band", "sub", None, None, None),
        P(("band", "sub"), None),
        P(("band", "sub"), None),
    )
    out_specs = (P("band", None, None), P("band", "sub", None, None, None))
    return jax.shard_map(
        functools.partial(body, nx, ny), mesh=mesh, in_specs=in_specs, out_specs=out_specs, check_vma=False
    )
```
